256 devices in a mesh: section: 8 (over y, core), slab: 32 (over x, z).
Axes of the slice: x: 4, y: 4, z: 8, core: 2. Of those that a mesh axis runs over, the one named last changes fastest.
Arguments:
- video_features: bfloat16 [2, 4, 64, 64, 256], P(None, None, 'slab'), may hold values from -6 to 6
- conv_weight: bfloat16 [8, 6912, 256], P('section'), may hold values from -0.078125 to 0.078125
- quant_weight: bfloat16 [256, 18], replicated, may hold values from -0.375 to 0.375
- post_weight: bfloat16 [18, 256], replicated, may hold values from -1.5 to 1.5
- latent_codes: int32 [2, 4, 64, 64], P(None, None, 'slab'), may hold values from 0 to 262143
- cotangent: bfloat16 [2, 4, 64, 64, 256], P(None, None, 'slab'), may hold values from -6 to 6
Outputs:
- section_output: bfloat16 [8, 2, 4, 64, 64, 256], P('section', None, None, 'slab')
- input_grad: bfloat16 [8, 2, 4, 64, 64, 256], P('section', None, None, 'slab')
- weight_grad: float32 [8, 6912, 256], P('section', 'slab')
The draws below stay inside these ranges and needn't reach their ends.
Inputs may be any that keep to these rules, and one draw needn't show every extreme that they name: `latent_codes`: its 18 binary digits, lowest first, are the lookup-free code bits of the position.
All inputs are finite; a program needn't handle non-finite values.
Results may differ from the reference program's by a relative error of at most 0.024.
Values may be sent and summed in bfloat16 or wider, within the bound.
No kernel may reach another device: no remote copies, remote signals or barrier semaphores. Data moves between devices by JAX's collectives and lax.ppermute only.
A program may use at most 128 MiB of HBM per device.

```python
import jax
import jax.numpy as jnp
from jax import lax

CH = 256
BITS = 18
FRAMES = 4
MICRO = 2
COLS = 64
HEIGHT = 64
LAYERS = 8
N_SECTION = 8


def plant(result, rng, least, largest):
    spot = [jax.random.randint(jax.random.fold_in(rng, axis), (), 0, length) for axis, length in enumerate(result.shape)]
    widest = result.shape.index(max(result.shape))
    next_to = spot[:widest] + [(spot[widest] + 1) % result.shape[widest]] + spot[widest + 1:]
    return result.at[tuple(spot)].set(least).at[tuple(next_to)].set(largest)


def levels(stream_key, extent, cuts, least, top_value):
    gain = 1.0
    for axis_at, parts in cuts:
        heights = jax.random.uniform(jax.random.fold_in(jax.random.fold_in(stream_key, 6), axis_at), (parts,), jnp.float32, least / len(cuts), top_value / len(cuts))
        gain = gain * jnp.repeat(jnp.exp(heights), extent[axis_at] // parts).reshape((-1,) + (1,) * (len(extent) - 1 - axis_at))
    return gain


def normal_values(rng, dims, width, reach, cuts=(), held_as=jnp.bfloat16):
    drawn = width * jax.random.normal(rng, dims, jnp.float32)
    if cuts:
        drawn = drawn * levels(rng, dims, cuts, -0.22, 0.18)
    return jnp.clip(drawn, -reach, reach).astype(held_as)


def setup_inputs(seed: int = 0) -> dict:
    streams_of = jax.random.split(jax.random.key(seed), 7)
    video_features = normal_values(streams_of[0], (MICRO, FRAMES, HEIGHT, COLS, CH), 1.0, 6.0, ((2, 32),))
    conv_weight = normal_values(streams_of[1], (LAYERS, 27 * CH, CH), (27 * CH) ** -0.5, 0.078125, ((0, 8),))
    quant_weight = normal_values(streams_of[2], (CH, BITS), CH ** -0.5, 0.375)
    post_weight = normal_values(streams_of[3], (BITS, CH), BITS ** -0.5, 1.5)
    latent_codes = plant(jax.random.randint(streams_of[4], (MICRO, FRAMES, HEIGHT, COLS), 0, 2 ** BITS), jax.random.fold_in(streams_of[4], 1), 0, (2 ** BITS) - 1).astype(jnp.int32)
    cotangent = normal_values(streams_of[5], (MICRO, FRAMES, HEIGHT, COLS, CH), 1.0, 6.0, ((2, 32),))
    return {"video_features": video_features, "conv_weight": conv_weight, "quant_weight": quant_weight, "post_weight": post_weight, "latent_codes": latent_codes, "cotangent": cotangent}


COMMIT = 0.25


def tap_matrix(padded, frames, row_count, col_count, flipped_order):
    pieces = []
    for offset_t in range(3):
        for offset_r in range(3):
            for offset_c in range(3):
                if flipped_order:
                    begin_t, begin_r, begin_c = 2 - offset_t, 2 - offset_r, 2 - offset_c
                else:
                    begin_t, begin_r, begin_c = offset_t, offset_r, offset_c
                pieces.append(padded[begin_t:begin_t + frames, begin_r:begin_r + row_count, begin_c:begin_c + col_count])
    stacked = jnp.stack(pieces, axis=-2)
    return stacked.reshape(frames * row_count * col_count, -1)


def reference(video_features, conv_weight, quant_weight, post_weight, latent_codes, cotangent):
    middle = N_SECTION // 2
    field_shape = (FRAMES, HEIGHT, COLS, CH)
    powers = 2 ** jnp.arange(BITS, dtype=jnp.int32)
    sign_table = ((latent_codes[..., None] // powers) % 2).astype(jnp.float32) * 2.0 - 1.0
    outputs_by_section = [[None] * MICRO for section in range(N_SECTION)]
    grads_by_section = [[None] * MICRO for section in range(N_SECTION)]
    weight_grads = [jnp.zeros((27 * CH, CH), jnp.float32) for section in range(N_SECTION)]
    for batch_index in range(MICRO):
        current = video_features[batch_index]
        sign_values = sign_table[batch_index].reshape(-1, BITS)
        inputs_list = []
        preact_list = []
        encoded = current
        for section in range(N_SECTION):
            if section == middle:
                encoded = current
                current = jnp.dot(sign_values.astype(jnp.bfloat16), post_weight, preferred_element_type=jnp.float32).astype(jnp.bfloat16).reshape(field_shape)
            padded = jnp.pad(current, ((2, 0), (1, 1), (1, 1), (0, 0)))
            preact = jnp.dot(tap_matrix(padded, FRAMES, HEIGHT, COLS, False), conv_weight[section], preferred_element_type=jnp.float32).reshape(field_shape)
            produced = (current.astype(jnp.float32) + jax.nn.silu(preact)).astype(jnp.bfloat16)
            inputs_list.append(padded)
            preact_list.append(preact)
            outputs_by_section[section][batch_index] = produced
            current = produced
        incoming = cotangent[batch_index]
        for section in range(N_SECTION - 1, -1, -1):
            preact = preact_list[section]
            sigmoid_u = jax.nn.sigmoid(preact)
            pre_grad = (incoming.astype(jnp.float32) * sigmoid_u * (1.0 + preact * (1.0 - sigmoid_u))).astype(jnp.bfloat16)
            columns = tap_matrix(inputs_list[section], FRAMES, HEIGHT, COLS, False)
            weight_grads[section] = weight_grads[section] + lax.dot_general(columns, pre_grad.reshape(-1, CH), (((0,), (0,)), ((), ())), preferred_element_type=jnp.float32)
            flipped = conv_weight[section].reshape(27, CH, CH).transpose(0, 2, 1).reshape(27 * CH, CH)
            beside_all = jnp.pad(pre_grad, ((0, 2), (1, 1), (1, 1), (0, 0)))
            back_term = jnp.dot(tap_matrix(beside_all, FRAMES, HEIGHT, COLS, True), flipped, preferred_element_type=jnp.float32).reshape(field_shape)
            plain_grad = (incoming.astype(jnp.float32) + back_term).astype(jnp.bfloat16)
            if section == middle:
                latent = jnp.dot(encoded.reshape(-1, CH), quant_weight, preferred_element_type=jnp.float32)
                latent_grad = jnp.dot(plain_grad.reshape(-1, CH), post_weight.T, preferred_element_type=jnp.float32) + 2.0 * COMMIT * (latent - sign_values)
                plain_grad = jnp.dot(latent_grad.astype(jnp.bfloat16), quant_weight.T, preferred_element_type=jnp.float32).astype(jnp.bfloat16).reshape(field_shape)
            grads_by_section[section][batch_index] = plain_grad
            incoming = plain_grad
    section_output = jnp.stack([jnp.stack(entries) for entries in outputs_by_section])
    input_grad = jnp.stack([jnp.stack(entries) for entries in grads_by_section])
    return section_output, input_grad, jnp.stack(weight_grads)
```

```python
import functools

import jax
import jax.numpy as jnp
from jax import lax
from jax.experimental import pallas as pl
from jax.experimental.pallas import tpu as pltpu
from jax.sharding import PartitionSpec as P

COMMIT = 0.25
BOTH = ("section", "slab")
CH = 256
WIDE = 3 * CH
LANES = 128
MIB = 1024 * 1024


def shifted(value, step):
    count, cols, channels = value.shape
    flat = value.astype(jnp.float32).reshape(count * cols, channels)
    rolled = pltpu.roll(flat, (-step) % (count * cols), 0)
    column = lax.broadcasted_iota(jnp.int32, (count * cols, 1), 0) % cols
    inside = column != (cols - 1 if step == 1 else 0)
    return jnp.where(inside, rolled, 0.0).astype(jnp.bfloat16).reshape(value.shape)


def spread(source, target, steps):
    for frame in range(source.shape[0]):
        value = source[frame]
        for third, step in enumerate(steps):
            target[frame, :, :, third * CH : (third + 1) * CH] = (
                value if step == 0 else shifted(value, step)
            )


def convolve(wide, weights, layer, total, rows, flipped, arrived):
    frames = wide.shape[0]
    cols = wide.shape[2]
    for offset_t in (2, 1, 0):
        count = frames - (2 - offset_t)
        lost = frames - count
        for offset_r in range(3):
            tap = 3 * offset_t + offset_r
            arrived(layer, tap)
            if flipped:
                lhs = wide[lost:frames, 2 - offset_r : 2 - offset_r + rows]
                place = slice(0, count)
            else:
                lhs = wide[0:count, offset_r : offset_r + rows]
                place = slice(lost, frames)
            part = jnp.dot(
                lhs.reshape(count * rows * cols, WIDE),
                weights[layer, tap * WIDE : (tap + 1) * WIDE, :],
                preferred_element_type=jnp.float32,
            ).reshape(count, rows, cols, CH)
            if offset_t == 2 and offset_r == 0:
                total[place, 0:rows] = part
            else:
                total[place, 0:rows] += part


def weight_copies(flags, own, other, held, sems):
    def copy(source, layer, tap):
        part = pl.ds(tap * WIDE, WIDE)
        return pltpu.make_async_copy(source.at[part], held.at[layer, part], sems.at[layer, tap])

    def start(order):
        for layer in order:
            for tap in (6, 7, 8, 3, 4, 5, 0, 1, 2):

                @pl.when(flags[1] == layer)
                def _():
                    copy(own, layer, tap).start()

                @pl.when(flags[1] != layer)
                def _():
                    copy(other, layer, tap).start()

    def arrived(layer, tap):
        copy(own, layer, tap).wait()

    return start, arrived


def inside_rows(flags, value, margin):
    rows = value.shape[1]
    index = lax.broadcasted_iota(jnp.int32, (1, rows, 1, 1), 1)
    outside = ((flags[2] == 1) & (index < margin)) | ((flags[3] == 1) & (index >= rows - margin))
    return jnp.where(outside, jnp.zeros_like(value), value)


def forward_kernel(flags, x_ref, own, other, ha, da, hb, db, held, wide, wide_b, total, sems):
    @pl.when(flags[0] == 1)
    def _():
        start, arrived = weight_copies(flags, own, other, held, sems)
        start((0, 1))

        def finish(rows, centre, keep_h, keep_d, mask):
            for frame in range(total.shape[0]):
                pre = total[frame, 0:rows]
                gate = 1.0 / (1.0 + jnp.exp(-pre))
                slope = gate * (1.0 + pre * (1.0 - gate))
                value = centre[frame, 1 : 1 + rows].astype(jnp.float32) + pre * gate
                value = value.astype(jnp.bfloat16)
                if mask:
                    for row, flag in ((0, 2), (rows - 1, 3)):
                        keep_h[frame, row] = jnp.where(
                            flags[flag] == 1, jnp.zeros_like(value[row]), value[row]
                        )
                    keep_h[frame, 1 : rows - 1] = value[1 : rows - 1]
                else:
                    keep_h[frame] = value
                keep_d[frame] = slope.astype(jnp.bfloat16)

        spread(x_ref, wide, (-1, 0, 1))
        convolve(wide, held, 0, total, 4, False, arrived)
        finish(4, x_ref, ha, da, True)
        spread(ha, wide_b, (-1, 0, 1))
        convolve(wide_b, held, 1, total, 2, False, arrived)
        finish(2, ha, hb, db, False)


def backward_kernel(
    flags, g_ref, db_ref, da_ref, own, other, post_t, commit, quant_t,
    pgb, igb, pga, iga,
    held, grad, wide, wide_b, plain, total, sems,
):
    frames, rows6, cols, channels = g_ref.shape

    @pl.when(flags[0] == 1)
    def _():
        start, arrived = weight_copies(flags, own, other, held, sems)
        start((1, 0))

        def gate_in(source, slope, target, margin):
            rows = source.shape[1]
            for frame in range(frames):
                for row in range(rows):
                    value = source[frame, row].astype(jnp.float32) * slope[frame, row].astype(
                        jnp.float32
                    )
                    value = value.astype(jnp.bfloat16)
                    if row < margin:
                        value = jnp.where(flags[2] == 1, jnp.zeros_like(value), value)
                    if row >= rows - margin:
                        value = jnp.where(flags[3] == 1, jnp.zeros_like(value), value)
                    target[frame, row] = value

        gate_in(g_ref, db_ref, grad, 2)
        pgb[...] = grad[:, 2:4]
        spread(grad, wide, (1, 0, -1))
        convolve(wide, held, 1, total, 4, True, arrived)
        for frame in range(frames):
            plain[frame] = (g_ref[frame, 1:5].astype(jnp.float32) + total[frame]).astype(
                jnp.bfloat16
            )
        igb[...] = plain[:, 1:3]
        small = grad.at[:, 0:4]
        gate_in(plain, da_ref, small, 1)
        pga[...] = grad[:, 1:3]
        spread(small, wide_b, (1, 0, -1))
        convolve(wide_b, held, 0, total, 2, True, arrived)
        for frame in range(frames):
            iga[frame] = (plain[frame, 1:3].astype(jnp.float32) + total[frame, 0:2]).astype(
                jnp.bfloat16
            )

        @pl.when(flags[4] == 1)
        def _():
            whole = iga[...].reshape(frames * 2 * cols, channels)
            latent_grad = (
                jnp.dot(whole, post_t[...], preferred_element_type=jnp.float32) + commit[...]
            )
            back = jnp.dot(
                latent_grad.astype(jnp.bfloat16), quant_t[...], preferred_element_type=jnp.float32
            )
            iga[...] = back.astype(jnp.bfloat16).reshape(iga.shape)


def weight_grad_kernel(x_ref, pg_ref, out, wide):
    frames, rows, cols, channels = pg_ref.shape
    spread(x_ref, wide, (-1, 0, 1))
    for offset_t in range(3):
        lost = 2 - offset_t
        rhs = pg_ref[lost:frames].reshape((frames - lost) * rows * cols, channels)
        for offset_r in range(3):
            lhs = wide[0 : frames - lost, offset_r : offset_r + rows]
            lhs = lhs.reshape((frames - lost) * rows * cols, WIDE)
            tap = 3 * offset_t + offset_r
            part = lax.dot_general(
                lhs, rhs, (((0,), (0,)), ((), ())), preferred_element_type=jnp.float32
            )
            out[tap * WIDE : (tap + 1) * WIDE, :] = part.astype(jnp.bfloat16)


VMEM = pl.BlockSpec(memory_space=pltpu.VMEM)
SMEM = pl.BlockSpec(memory_space=pltpu.SMEM)
ANY = pl.BlockSpec(memory_space=pl.ANY)


def bf16(*shape):
    return jax.ShapeDtypeStruct(shape, jnp.bfloat16)


def cost(rows, cols, frames):
    flops = 2 * 27 * CH * CH * rows * cols * frames
    return pl.CostEstimate(flops=flops, bytes_accessed=4 * 27 * CH * CH, transcendentals=0)


def forward_pair(flags, x6, own, other):
    frames, rows, cols, channels = x6.shape
    depth = own.shape[0]
    return pl.pallas_call(
        forward_kernel,
        out_shape=(
            bf16(frames, 4, cols, channels),
            bf16(frames, 4, cols, channels),
            bf16(frames, 2, cols, channels),
            bf16(frames, 2, cols, channels),
        ),
        in_specs=[SMEM, VMEM, ANY, ANY],
        out_specs=(VMEM,) * 4,
        scratch_shapes=[
            pltpu.VMEM((2, depth, channels), jnp.bfloat16),
            pltpu.VMEM((frames, 6, cols, WIDE), jnp.bfloat16),
            pltpu.VMEM((frames, 4, cols, WIDE), jnp.bfloat16),
            pltpu.VMEM((frames, 4, cols, channels), jnp.float32),
            pltpu.SemaphoreType.DMA((2, 9)),
        ],
        compiler_params=pltpu.CompilerParams(vmem_limit_bytes=32 * MIB),
        cost_estimate=cost(6, cols, frames),
    )(flags, x6, own, other)


def backward_pair(flags, g6, db6, da4, own, other, post_t, commit, quant_t):
    frames, rows, cols, channels = g6.shape
    depth = own.shape[0]
    return pl.pallas_call(
        backward_kernel,
        out_shape=(bf16(frames, 2, cols, channels),) * 4,
        in_specs=[SMEM, VMEM, VMEM, VMEM, ANY, ANY, VMEM, VMEM, VMEM],
        out_specs=(VMEM,) * 4,
        scratch_shapes=[
            pltpu.VMEM((2, depth, channels), jnp.bfloat16),
            pltpu.VMEM((frames, 6, cols, channels), jnp.bfloat16),
            pltpu.VMEM((frames, 6, cols, WIDE), jnp.bfloat16),
            pltpu.VMEM((frames, 4, cols, WIDE), jnp.bfloat16),
            pltpu.VMEM((frames, 4, cols, channels), jnp.bfloat16),
            pltpu.VMEM((frames, 4, cols, channels), jnp.float32),
            pltpu.SemaphoreType.DMA((2, 9)),
        ],
        compiler_params=pltpu.CompilerParams(vmem_limit_bytes=32 * MIB),
        cost_estimate=cost(6, cols, frames),
    )(flags, g6, db6, da4, own, other, post_t, commit, quant_t)


def weight_grad_of(x4, pg):
    frames, rows, cols, channels = pg.shape
    return pl.pallas_call(
        weight_grad_kernel,
        out_shape=bf16(27 * channels, channels),
        in_specs=[VMEM, VMEM],
        out_specs=VMEM,
        scratch_shapes=[pltpu.VMEM((frames, 4, cols, WIDE), jnp.bfloat16)],
        compiler_params=pltpu.CompilerParams(vmem_limit_bytes=24 * MIB),
        cost_estimate=cost(2, cols, frames),
    )(x4, pg)


def body(video_features, conv_weight, quant_weight, post_weight, latent_codes, cotangent):
    sections = lax.axis_size("section")
    slabs = lax.axis_size("slab")
    position = lax.axis_index("section")
    slab = lax.axis_index("slab")
    plane = position // 2
    core = position % 2
    planes = sections // 2
    middle = planes // 2
    micro_count, frames, row_count, cols, channels = video_features.shape
    bit_count = quant_weight.shape[1]

    def to_slab(value, step):
        return lax.ppermute(value, "slab", [(i, (i + step) % slabs) for i in range(slabs)])

    def to_core(value):
        return lax.ppermute(value, "section", [(i, i ^ 1) for i in range(sections)])

    def across(value, from_planes, plane_step, slab_step):
        pairs = []
        for at in from_planes:
            for half in range(2):
                for i in range(slabs):
                    target = i + slab_step
                    if 0 <= target < slabs:
                        source_section = 2 * at + half
                        target_section = 2 * (at + plane_step) + half
                        pairs.append(
                            (source_section * slabs + i, target_section * slabs + target)
                        )
        return lax.ppermute(value, BOTH, pairs)

    def joined(low, value, high):
        low = jnp.where(slab == 0, jnp.zeros_like(low), low)
        high = jnp.where(slab == slabs - 1, jnp.zeros_like(high), high)
        return jnp.concatenate([low, value, high], axis=1)

    def beside(value):
        return joined(to_slab(value, 1), value, to_slab(value, -1))

    def crossed(value, from_planes, plane_step):
        main = across(value, from_planes, plane_step, 0)
        low = across(value, from_planes, plane_step, 1)
        high = across(value, from_planes, plane_step, -1)
        return joined(low, main, high)

    def flags_for(active):
        return jnp.stack(
            [
                active.astype(jnp.int32),
                core.astype(jnp.int32),
                (slab == 0).astype(jnp.int32),
                (slab == slabs - 1).astype(jnp.int32),
                (plane == middle).astype(jnp.int32),
            ]
        )

    own = conv_weight[0]
    other = to_core(own)

    codes = lax.dynamic_index_in_dim(latent_codes, core, 0, keepdims=False)
    bits = jnp.arange(32, dtype=jnp.int32)[:, None]
    flat_codes = codes.reshape(1, -1)
    sign_t = ((flat_codes >> bits) & 1).astype(jnp.float32) * 2.0 - 1.0
    sign_t = jnp.where(bits < bit_count, sign_t, 0.0)
    post_rows = jnp.pad(post_weight, ((0, 32 - bit_count), (0, 0)))
    dequant = (
        lax.dot_general(
            sign_t.astype(jnp.bfloat16),
            post_rows,
            (((0,), (0,)), ((), ())),
            preferred_element_type=jnp.float32,
        )
        .astype(jnp.bfloat16)
        .reshape(frames, row_count, cols, channels)
    )
    features = lax.dynamic_index_in_dim(video_features, core, 0, keepdims=False)
    upstream = lax.dynamic_index_in_dim(cotangent, core, 0, keepdims=False)
    entry = jnp.where(
        plane == middle, dequant, jnp.where(plane == planes - 1, upstream, features)
    )
    entry6 = beside(entry)

    first_half = (plane % 2) == 0
    ha0, da0, hb0, db0 = forward_pair(flags_for(first_half), entry6, own, other)
    passed6 = crossed(hb0, (0, 2), 1)
    ha1, da1, hb1, db1 = forward_pair(flags_for(~first_half), passed6, own, other)

    def pick(zero, one):
        return jnp.where(first_half, zero, one)

    x6, ha, da, hb, db = (
        pick(entry6, passed6), pick(ha0, ha1), pick(da0, da1), pick(hb0, hb1), pick(db0, db1)
    )
    encoded = across(hb1, (middle - 1,), 1, 0)
    db6 = beside(db)

    own_t = own.reshape(27, channels, channels).transpose(0, 2, 1).reshape(own.shape)
    other_t = to_core(own_t)
    post_t = jnp.pad(post_weight.T, ((0, 0), (0, LANES - bit_count)))
    quant_t = jnp.pad(quant_weight.T, ((0, LANES - bit_count), (0, 0)))
    quant_wide = jnp.pad(quant_weight, ((0, 0), (0, LANES - bit_count)))
    latent = jnp.dot(
        encoded.reshape(-1, channels), quant_wide, preferred_element_type=jnp.float32
    )
    sign_rows = jnp.pad(sign_t.T, ((0, 0), (0, LANES - 32)))
    commit = 2.0 * COMMIT * (latent - sign_rows)

    g6 = entry6
    kept = None
    for at in range(planes - 1, -1, -1):
        active = plane == at
        results = backward_pair(
            flags_for(active), g6, db6, da, own_t, other_t, post_t, commit, quant_t
        )
        kept = results if kept is None else tuple(
            jnp.where(active, new, old) for new, old in zip(results, kept)
        )
        if at > 0:
            g6 = crossed(results[3], (at,), -1)
    pgb, igb, pga, iga = kept

    def mine(value_a, value_b):
        keep = jnp.where(core == 0, value_a, value_b)
        send = jnp.where(core == 0, value_b, value_a)
        got = to_core(send)
        return jnp.stack([jnp.where(core == 0, keep, got), jnp.where(core == 0, got, keep)])

    section_output = mine(ha[:, 1:3], hb)
    input_grad = mine(iga, igb)

    x4 = x6[:, 1:5]
    send_x, keep_x = (jnp.where(core == 0, ha, x4), jnp.where(core == 0, x4, ha))
    send_pg, keep_pg = (jnp.where(core == 0, pgb, pga), jnp.where(core == 0, pga, pgb))
    sent = to_core(weight_grad_of(send_x, send_pg))
    held = weight_grad_of(keep_x, keep_pg)
    share = (held.astype(jnp.float32) + sent.astype(jnp.float32)).astype(jnp.bfloat16)
    along_x, along_z = 4, slabs // 4
    x_groups = [[x * along_z + z for x in range(along_x)] for z in range(along_z)]
    z_groups = [[x * along_z + z for z in range(along_z)] for x in range(along_x)]
    for count, groups, kind in ((along_x, x_groups, jnp.bfloat16), (along_z, z_groups, jnp.float32)):
        depth = share.shape[0] // count
        spread_out = lax.all_to_all(
            share, "slab", 0, 0, axis_index_groups=groups, tiled=True
        ).reshape(count, depth, channels)
        share = spread_out.astype(jnp.float32).sum(0).astype(kind)
    return (section_output[None], input_grad[None], share[None])


def solution(mesh):
    return jax.shard_map(
        body,
        mesh=mesh,
        in_specs=(
            P(None, None, "slab", None, None),
            P("section", None, None),
            P(),
            P(),
            P(None, None, "slab", None),
            P(None, None, "slab", None, None),
        ),
        out_specs=(
            P("section", None, None, "slab", None, None),
            P("section", None, None, "slab", None, None),
            P("section", "slab", None),
        ),
        check_vma=False,
    )
```

```python
import functools

import jax
import jax.numpy as jnp
from jax import lax
from jax.experimental import pallas as pl
from jax.experimental.pallas import tpu as pltpu
from jax.sharding import PartitionSpec as P

COMMIT = 0.25
BOTH = ("section", "slab")
CH = 256
WIDE = 3 * CH
LANES = 128
MIB = 1024 * 1024


def shifted(value, step):
    count, cols, channels = value.shape
    flat = value.astype(jnp.float32).reshape(count * cols, channels)
    rolled = pltpu.roll(flat, (-step) % (count * cols), 0)
    column = lax.broadcasted_iota(jnp.int32, (count * cols, 1), 0) % cols
    inside = column != (cols - 1 if step == 1 else 0)
    return jnp.where(inside, rolled, 0.0).astype(jnp.bfloat16).reshape(value.shape)


def each(count, function):
    def step(index, carry):
        function(index)
        return carry

    lax.fori_loop(0, count, step, 0)


def spread(source, target, steps):
    def one(frame):
        value = source[frame]
        for third, step in enumerate(steps):
            target[frame, :, :, third * CH : (third + 1) * CH] = (
                value if step == 0 else shifted(value, step)
            )

    each(source.shape[0], one)


def convolve(wide, weights, layer, rows, flipped, arrived, consume):
    frames, _, cols, _ = wide.shape
    order = range(frames - 1, -1, -1) if flipped else range(frames)
    for step, frame in enumerate(order):
        if step < 3:
            arrived(layer, 2 - step)
        first_t = max(0, 2 - step)
        pieces = []
        for offset_t in range(first_t, 3):
            source = frame - offset_t + 2 if flipped else frame + offset_t - 2
            for offset_r in range(3):
                begin = 2 - offset_r if flipped else offset_r
                pieces.append(wide[source, begin : begin + rows].reshape(rows * cols, WIDE))
        sums = jnp.dot(
            jnp.concatenate(pieces, axis=-1),
            weights[layer, first_t * 3 * WIDE : 9 * WIDE, :],
            preferred_element_type=jnp.float32,
        )
        consume(frame, sums.reshape(rows, cols, CH))


def weight_copies(flags, own, other, held, sems):
    def copy(source, layer, offset_t):
        part = pl.ds(offset_t * 3 * WIDE, 3 * WIDE)
        return pltpu.make_async_copy(
            source.at[part], held.at[layer, part], sems.at[layer, offset_t]
        )

    def start(order):
        for layer in order:
            for source, wanted in ((own, True), (other, False)):

                @pl.when((flags[1] == layer) == wanted)
                def _():
                    for offset_t in (2, 1, 0):
                        copy(source, layer, offset_t).start()

    def arrived(layer, offset_t):
        copy(own, layer, offset_t).wait()

    return start, arrived


def place_rows(low, main, high, target, sems, first):
    return [
        pltpu.make_async_copy(source, target.at[:, 2 * index : 2 * index + 2], sems.at[first + index])
        for index, source in enumerate((low, main, high))
    ]


def start_all(copies):
    for copy in copies:
        copy.start()


def wait_all(copies):
    for copy in copies:
        copy.wait()


def forward_kernel(flags, low, main, high, own, other, *refs):
    outs, scratch = refs[-15:-10], refs[-10:]
    x4_out, ha_out, da_out, hb_out, db_out = outs
    held, x, ha, da, hb, db, wide, wide_b, sems, moves = scratch

    @pl.when(flags[0] == 1)
    def _():
        rows_in = place_rows(low, main, high, x, moves, 0)
        start_all(rows_in)
        start, arrived = weight_copies(flags, own, other, held, sems)
        start((0, 1))
        wait_all(rows_in)
        for flag, first in ((2, 0), (3, 4)):

            @pl.when(flags[flag] == 1)
            def _():
                x[:, first : first + 2] = jnp.zeros_like(x[:, first : first + 2])

        def finish(rows, centre, keep_h, keep_d, mask):
            def one(frame, pre):
                gate = 1.0 / (1.0 + jnp.exp(-pre))
                slope = gate * (1.0 + pre * (1.0 - gate))
                value = centre[frame, 1 : 1 + rows].astype(jnp.float32) + pre * gate
                value = value.astype(jnp.bfloat16)
                if mask:
                    for row, flag in ((0, 2), (rows - 1, 3)):
                        keep_h[frame, row] = jnp.where(
                            flags[flag] == 1, jnp.zeros_like(value[row]), value[row]
                        )
                    keep_h[frame, 1 : rows - 1] = value[1 : rows - 1]
                else:
                    keep_h[frame] = value
                keep_d[frame] = slope.astype(jnp.bfloat16)

            return one

        spread(x, wide, (-1, 0, 1))
        convolve(wide, held, 0, 4, False, arrived, finish(4, x, ha, da, True))
        out_a = [
            pltpu.make_async_copy(x.at[:, 1:5], x4_out, moves.at[3]),
            pltpu.make_async_copy(ha, ha_out, moves.at[4]),
            pltpu.make_async_copy(da, da_out, moves.at[5]),
        ]
        start_all(out_a)
        spread(ha, wide_b, (-1, 0, 1))
        convolve(wide_b, held, 1, 2, False, arrived, finish(2, ha, hb, db, False))
        out_b = [
            pltpu.make_async_copy(hb, hb_out, moves.at[6]),
            pltpu.make_async_copy(db, db_out, moves.at[7]),
        ]
        start_all(out_b)
        wait_all(out_a + out_b)


def backward_kernel(
    flags, g_low, g_main, g_high, d_low, d_main, d_high, da_in, own, other, post_t, commit, quant_t,
    *refs,
):
    outs, scratch = refs[-16:-12], refs[-12:]
    pgb_out, igb_out, pga_out, iga_out = outs
    held, g, db, da, grad, small, plain, iga, wide, wide_b, sems, moves = scratch
    frames, rows6, cols, channels = g.shape

    @pl.when(flags[0] == 1)
    def _():
        rows_in = place_rows(g_low, g_main, g_high, g, moves, 0)
        rows_in += place_rows(d_low, d_main, d_high, db, moves, 3)
        slope_in = pltpu.make_async_copy(da_in, da, moves.at[6])
        start_all(rows_in)
        start, arrived = weight_copies(flags, own, other, held, sems)
        start((1, 0))
        slope_in.start()
        wait_all(rows_in)

        def gate_in(source, slope, target, margin):
            rows = source.shape[1]

            def one(frame):
                for row in range(rows):
                    value = source[frame, row].astype(jnp.float32) * slope[frame, row].astype(
                        jnp.float32
                    )
                    value = value.astype(jnp.bfloat16)
                    if row < margin:
                        value = jnp.where(flags[2] == 1, jnp.zeros_like(value), value)
                    if row >= rows - margin:
                        value = jnp.where(flags[3] == 1, jnp.zeros_like(value), value)
                    target[frame, row] = value

            each(frames, one)

        gate_in(g, db, grad, 2)
        spread(grad, wide, (1, 0, -1))

        def plain_b(frame, sums):
            plain[frame] = (g[frame, 1:5].astype(jnp.float32) + sums).astype(jnp.bfloat16)

        convolve(wide, held, 1, 4, True, arrived, plain_b)
        slope_in.wait()
        gate_in(plain, da, small, 1)
        early = [
            pltpu.make_async_copy(grad.at[:, 2:4], pgb_out, moves.at[7]),
            pltpu.make_async_copy(plain.at[:, 1:3], igb_out, moves.at[8]),
            pltpu.make_async_copy(small.at[:, 1:3], pga_out, moves.at[9]),
        ]
        start_all(early)
        spread(small, wide_b, (1, 0, -1))

        def plain_a(frame, sums):
            iga[frame] = (plain[frame, 1:3].astype(jnp.float32) + sums).astype(jnp.bfloat16)

        convolve(wide_b, held, 0, 2, True, arrived, plain_a)

        @pl.when(flags[4] == 1)
        def _():
            whole = iga[...].reshape(frames * 2 * cols, channels)
            latent_grad = (
                jnp.dot(whole, post_t[...], preferred_element_type=jnp.float32) + commit[...]
            )
            back = jnp.dot(
                latent_grad.astype(jnp.bfloat16), quant_t[...], preferred_element_type=jnp.float32
            )
            iga[...] = back.astype(jnp.bfloat16).reshape(iga.shape)

        last = pltpu.make_async_copy(iga, iga_out, moves.at[10])
        last.start()
        wait_all(early + [last])


def weight_grad_kernel(place, x_gathered, *refs):
    x_all, beside, total, moves = refs[-4:]
    out = refs[-5]
    count = len(refs) - 5
    pg_parts = refs[:count]
    clips, frames, rows, cols, channels = beside.shape[1:]
    group = clips // count
    pg_in, x_in = [], []
    for index in range(count):
        clip = slice(index * group, (index + 1) * group)
        pg_in.append(pltpu.make_async_copy(pg_parts[index], beside.at[1, clip], moves.at[index]))
        x_in.append(
            pltpu.make_async_copy(
                x_gathered.at[place[2 + index]],
                x_all.at[clip, 2 : 2 + frames],
                moves.at[count + index],
            )
        )
    start_all(pg_in + x_in)
    x_all[:, 0:2] = jnp.zeros_like(x_all[:, 0:2])
    for index in range(count):
        pg_in[index].wait()

        def one(at):
            clip, frame = index * group + at // frames, at % frames
            value = beside[1, clip, frame]
            beside[0, clip, frame] = shifted(value, 1)
            beside[2, clip, frame] = shifted(value, -1)

        each(group * frames, one)
    wait_all(x_in)

    def one_tap(number):
        tap = jnp.minimum(place[0] + number, 26)
        offset_t, offset_r, offset_c = tap // 9, (tap // 3) % 3, tap % 3
        depth = clips * frames * rows * cols
        lhs = x_all[:, pl.ds(offset_t, frames), pl.ds(offset_r, rows)].reshape(depth, channels)
        rhs = beside[offset_c].reshape(depth, channels)
        total[pl.ds(pl.multiple_of(number * channels, channels), channels), :] = lax.dot_general(
            lhs, rhs, (((0,), (0,)), ((), ())), preferred_element_type=jnp.float32
        )

    each(8, one_tap)
    begin = pl.multiple_of(place[1], 64)
    out[...] = total[pl.ds(begin, out.shape[0]), :].astype(jnp.bfloat16)


VMEM = pl.BlockSpec(memory_space=pltpu.VMEM)
SMEM = pl.BlockSpec(memory_space=pltpu.SMEM)
HBM = pl.BlockSpec(memory_space=pltpu.HBM)


def bf16(*shape):
    return jax.ShapeDtypeStruct(shape, jnp.bfloat16)


def cost(rows, cols, frames):
    flops = 2 * 27 * CH * CH * rows * cols * frames
    return pl.CostEstimate(flops=flops, bytes_accessed=4 * 27 * CH * CH, transcendentals=0)


def forward_pair(flags, rows, own, other, kept=()):
    frames, _, cols, channels = rows[1].shape
    depth = own.shape[0]
    four, two = (frames, 4, cols, channels), (frames, 2, cols, channels)
    return pl.pallas_call(
        forward_kernel,
        out_shape=(bf16(*four), bf16(*four), bf16(*four), bf16(*two), bf16(*two)),
        in_specs=[SMEM] + [HBM] * (5 + len(kept)),
        out_specs=(HBM,) * 5,
        input_output_aliases={6 + index: index for index in range(len(kept))},
        scratch_shapes=[
            pltpu.VMEM((2, depth, channels), jnp.bfloat16),
            pltpu.VMEM((frames, 6, cols, channels), jnp.bfloat16),
            pltpu.VMEM(four, jnp.bfloat16),
            pltpu.VMEM(four, jnp.bfloat16),
            pltpu.VMEM(two, jnp.bfloat16),
            pltpu.VMEM(two, jnp.bfloat16),
            pltpu.VMEM((frames, 6, cols, WIDE), jnp.bfloat16),
            pltpu.VMEM((frames, 4, cols, WIDE), jnp.bfloat16),
            pltpu.SemaphoreType.DMA((2, 3)),
            pltpu.SemaphoreType.DMA((8,)),
        ],
        compiler_params=pltpu.CompilerParams(vmem_limit_bytes=60 * MIB),
        cost_estimate=cost(6, cols, frames),
    )(flags, *rows, own, other, *kept)


def backward_pair(flags, g_rows, d_rows, da, own, other, post_t, commit, quant_t, kept=()):
    frames, _, cols, channels = g_rows[1].shape
    depth = own.shape[0]
    six, four, two = ((frames, count, cols, channels) for count in (6, 4, 2))
    return pl.pallas_call(
        backward_kernel,
        out_shape=(bf16(*two),) * 4,
        in_specs=[SMEM] + [HBM] * 9 + [VMEM] * 3 + [HBM] * len(kept),
        out_specs=(HBM,) * 4,
        input_output_aliases={13 + index: index for index in range(len(kept))},
        scratch_shapes=[
            pltpu.VMEM((2, depth, channels), jnp.bfloat16),
            pltpu.VMEM(six, jnp.bfloat16),
            pltpu.VMEM(six, jnp.bfloat16),
            pltpu.VMEM(four, jnp.bfloat16),
            pltpu.VMEM(six, jnp.bfloat16),
            pltpu.VMEM(four, jnp.bfloat16),
            pltpu.VMEM(four, jnp.bfloat16),
            pltpu.VMEM(two, jnp.bfloat16),
            pltpu.VMEM((frames, 6, cols, WIDE), jnp.bfloat16),
            pltpu.VMEM((frames, 4, cols, WIDE), jnp.bfloat16),
            pltpu.SemaphoreType.DMA((2, 3)),
            pltpu.SemaphoreType.DMA((11,)),
        ],
        compiler_params=pltpu.CompilerParams(vmem_limit_bytes=60 * MIB),
        cost_estimate=cost(6, cols, frames),
    )(flags, *g_rows, *d_rows, da, own, other, post_t, commit, quant_t, *kept)


def weight_grad_part(place, x_gathered, pg_parts, depth):
    frames, rows, cols, channels = pg_parts[0].shape[1:]
    clips = pg_parts[0].shape[0] * len(pg_parts)
    return pl.pallas_call(
        weight_grad_kernel,
        out_shape=bf16(depth, channels),
        in_specs=[SMEM] + [HBM] * (1 + len(pg_parts)),
        out_specs=VMEM,
        scratch_shapes=[
            pltpu.VMEM((clips, frames + 2, rows + 2, cols, channels), jnp.bfloat16),
            pltpu.VMEM((3, clips, frames, rows, cols, channels), jnp.bfloat16),
            pltpu.VMEM((8 * channels, channels), jnp.float32),
            pltpu.SemaphoreType.DMA((2 * len(pg_parts),)),
        ],
        compiler_params=pltpu.CompilerParams(vmem_limit_bytes=60 * MIB),
        cost_estimate=cost(2, cols, 2 * frames),
    )(place, x_gathered, *pg_parts)


def body(video_features, conv_weight, quant_weight, post_weight, latent_codes, cotangent):
    sections = lax.axis_size("section")
    slabs = lax.axis_size("slab")
    position = lax.axis_index("section")
    slab = lax.axis_index("slab")
    plane = position // 2
    core = position % 2
    planes = sections // 2
    middle = planes // 2
    micro_count, frames, row_count, cols, channels = video_features.shape
    bit_count = quant_weight.shape[1]

    def to_slab(value, step):
        return lax.ppermute(value, "slab", [(i, (i + step) % slabs) for i in range(slabs)])

    def to_core(value):
        return lax.ppermute(value, "section", [(i, i ^ 1) for i in range(sections)])

    def across(value, from_planes, plane_step, slab_step):
        pairs = []
        for at in from_planes:
            for half in range(2):
                for i in range(slabs):
                    target = i + slab_step
                    if 0 <= target < slabs:
                        source_section = 2 * at + half
                        target_section = 2 * (at + plane_step) + half
                        pairs.append(
                            (source_section * slabs + i, target_section * slabs + target)
                        )
        return lax.ppermute(value, BOTH, pairs)

    def beside(value):
        return to_slab(value, 1), value, to_slab(value, -1)

    def crossed(value, from_planes, plane_step):
        return tuple(across(value, from_planes, plane_step, step) for step in (1, 0, -1))

    def flags_for(active):
        return jnp.stack(
            [
                active.astype(jnp.int32),
                core.astype(jnp.int32),
                (slab == 0).astype(jnp.int32),
                (slab == slabs - 1).astype(jnp.int32),
                (plane == middle).astype(jnp.int32),
            ]
        )

    own = conv_weight[0]
    other = to_core(own)

    codes = lax.dynamic_index_in_dim(latent_codes, core, 0, keepdims=False)
    bits = jnp.arange(32, dtype=jnp.int32)[:, None]
    flat_codes = codes.reshape(1, -1)
    sign_t = ((flat_codes >> bits) & 1).astype(jnp.float32) * 2.0 - 1.0
    sign_t = jnp.where(bits < bit_count, sign_t, 0.0)
    post_rows = jnp.pad(post_weight, ((0, 32 - bit_count), (0, 0)))
    dequant = (
        lax.dot_general(
            sign_t.astype(jnp.bfloat16),
            post_rows,
            (((0,), (0,)), ((), ())),
            preferred_element_type=jnp.float32,
        )
        .astype(jnp.bfloat16)
        .reshape(frames, row_count, cols, channels)
    )
    features = lax.dynamic_index_in_dim(video_features, core, 0, keepdims=False)
    upstream = lax.dynamic_index_in_dim(cotangent, core, 0, keepdims=False)
    entry = jnp.where(
        plane == middle, dequant, jnp.where(plane == planes - 1, upstream, features)
    )
    entry_rows = beside(entry)
    post_t = jnp.pad(post_weight.T, ((0, 0), (0, LANES - bit_count)))
    quant_t = jnp.pad(quant_weight.T, ((0, LANES - bit_count), (0, 0)))
    quant_wide = jnp.pad(quant_weight, ((0, 0), (0, LANES - bit_count)))
    sign_rows = jnp.pad(sign_t.T, ((0, 0), (0, LANES - 32)))

    first_half = (plane % 2) == 0
    flags = [flags_for(plane == at) for at in range(planes)]
    even, odd = flags_for(first_half), flags_for(~first_half)
    entry_rows, post_t, quant_t, quant_wide, sign_rows, flags, even, odd = lax.optimization_barrier(
        (entry_rows, post_t, quant_t, quant_wide, sign_rows, flags, even, odd)
    )
    stage = forward_pair(even, entry_rows, own, other)
    passed = crossed(stage[3], (0, 2), 1)
    own_late, _ = lax.optimization_barrier((own, stage[3]))
    own_t = own_late.reshape(27, channels, channels).transpose(0, 2, 1).reshape(own.shape)
    x4, ha, da, hb, db = forward_pair(odd, passed, own, other, stage)
    d_rows = beside(db)
    hb_late, _ = lax.optimization_barrier((hb, d_rows))
    encoded = across(hb_late, (middle - 1,), 1, 0)
    other_t = to_core(own_t)

    along_x, along_z = 4, slabs // 4

    def mine(value_a, value_b):
        keep = jnp.where(core == 0, value_a, value_b)
        send = jnp.where(core == 0, value_b, value_a)
        got = to_core(send)
        return jnp.stack([jnp.where(core == 0, keep, got), jnp.where(core == 0, got, keep)])

    def along_ring(value):
        gathered = [value]
        for step in (1, along_x - 1, 2):
            route = [(i, (i + step * along_z) % slabs) for i in range(slabs)]
            gathered.append(lax.ppermute(value, "slab", route))
        return gathered

    x_mine = mine(x4, ha)
    d_rows, x_mine = lax.optimization_barrier((d_rows, x_mine))
    x_groups = [[x * along_z + z for x in range(along_x)] for z in range(along_z)]
    x_all = lax.all_gather(x_mine, "slab", axis_index_groups=x_groups)

    latent = jnp.dot(
        encoded.reshape(-1, channels), quant_wide, preferred_element_type=jnp.float32
    )
    commit = 2.0 * COMMIT * (latent - sign_rows)

    g_rows = entry_rows
    kept = ()
    for at in range(planes - 1, -1, -1):
        kept = backward_pair(
            flags[at], g_rows, d_rows, da, own_t, other_t, post_t, commit, quant_t, kept
        )
        if at > 0:
            g_rows = crossed(kept[3], (at,), -1)
    pgb, igb, pga, iga = kept

    pg_parts = along_ring(mine(pga, pgb))
    section_output = mine(ha[:, 1:3], hb)
    input_grad = mine(iga, igb)
    depth = own.shape[0] // along_x
    first_row = (slab // along_z) * depth
    sources = [(slab // along_z + along_x - step) % along_x for step in (0, 1, along_x - 1, 2)]
    place = jnp.stack([first_row // channels, first_row % channels] + sources).astype(jnp.int32)
    share = weight_grad_part(place, x_all, pg_parts, depth)
    z_groups = [[x * along_z + z for z in range(along_z)] for x in range(along_x)]
    share = (
        lax.all_to_all(share, "slab", 0, 0, axis_index_groups=z_groups, tiled=True)
        .reshape(along_z, depth // along_z, channels)
        .astype(jnp.float32)
        .sum(0)
    )
    return (section_output[None], input_grad[None], share[None])


def solution(mesh):
    return jax.shard_map(
        body,
        mesh=mesh,
        in_specs=(
            P(None, None, "slab", None, None),
            P("section", None, None),
            P(),
            P(),
            P(None, None, "slab", None),
            P(None, None, "slab", None, None),
        ),
        out_specs=(
            P("section", None, None, "slab", None, None),
            P("section", None, None, "slab", None, None),
            P("section", "slab", None),
        ),
        check_vma=False,
    )
```

```python
import functools

import jax
import jax.numpy as jnp
from jax import lax
from jax.experimental import pallas as pl
from jax.experimental.pallas import tpu as pltpu
from jax.sharding import PartitionSpec as P

COMMIT = 0.25
BOTH = ("section", "slab")
CH = 256
WIDE = 3 * CH
LANES = 128
MIB = 1024 * 1024


def shifted(value, step):
    count, cols, channels = value.shape
    flat = value.astype(jnp.float32).reshape(count * cols, channels)
    rolled = pltpu.roll(flat, (-step) % (count * cols), 0)
    column = lax.broadcasted_iota(jnp.int32, (count * cols, 1), 0) % cols
    inside = column != (cols - 1 if step == 1 else 0)
    return jnp.where(inside, rolled, 0.0).astype(jnp.bfloat16).reshape(value.shape)


def each(count, function):
    def step(index, carry):
        function(index)
        return carry

    lax.fori_loop(0, count, step, 0)


def spread(source, target, steps):
    def one(frame):
        value = source[frame]
        for third, step in enumerate(steps):
            target[frame, :, :, third * CH : (third + 1) * CH] = (
                value if step == 0 else shifted(value, step)
            )

    each(source.shape[0], one)


def convolve(wide, weights, layer, rows, flipped, arrived, consume):
    frames, _, cols, _ = wide.shape
    order = range(frames - 1, -1, -1) if flipped else range(frames)
    for step, frame in enumerate(order):
        if step < 3:
            arrived(layer, 2 - step)
        first_t = max(0, 2 - step)
        pieces = []
        for offset_t in range(first_t, 3):
            source = frame - offset_t + 2 if flipped else frame + offset_t - 2
            for offset_r in range(3):
                begin = 2 - offset_r if flipped else offset_r
                pieces.append(wide[source, begin : begin + rows].reshape(rows * cols, WIDE))
        sums = jnp.dot(
            jnp.concatenate(pieces, axis=-1),
            weights[layer, first_t * 3 * WIDE : 9 * WIDE, :],
            preferred_element_type=jnp.float32,
        )
        consume(frame, sums.reshape(rows, cols, CH))


def weight_copies(flags, at, own, other, held, sems):
    def copy(source, layer, offset_t):
        part = pl.ds(offset_t * 3 * WIDE, 3 * WIDE)
        return pltpu.make_async_copy(
            source.at[part], held.at[layer, part], sems.at[layer, offset_t]
        )

    def start(order):
        for layer in order:
            for source, wanted in ((own, True), (other, False)):

                @pl.when((flags[at, 1] == layer) == wanted)
                def _():
                    for offset_t in (2, 1, 0):
                        copy(source, layer, offset_t).start()

    def arrived(layer, offset_t):
        copy(own, layer, offset_t).wait()

    return start, arrived


def place_rows(low, main, high, target, sems, first):
    return [
        pltpu.make_async_copy(source, target.at[:, 2 * index : 2 * index + 2], sems.at[first + index])
        for index, source in enumerate((low, main, high))
    ]


def sorted_copies(first, second, keep, send, sems, at):
    return [
        [
            pltpu.make_async_copy(first, target, sems.at[at]),
            pltpu.make_async_copy(second, partner, sems.at[at + 1]),
        ]
        for target, partner in ((keep, send), (send, keep))
    ]


def start_sorted(choices, core):
    for index, copies in enumerate(choices):

        @pl.when(core == index)
        def _():
            start_all(copies)


def start_all(copies):
    for copy in copies:
        copy.start()


def wait_all(copies):
    for copy in copies:
        copy.wait()


def forward_kernel(at, flags, low, main, high, own, other, *refs):
    outs, scratch = refs[-17:-10], refs[-10:]
    x_keep, x_send, out_keep, out_send, da_out, hb_out, db_out = outs
    held, x, ha, da, hb, db, wide, wide_b, sems, moves = scratch

    @pl.when(flags[at, 0] == 1)
    def _():
        rows_in = place_rows(low, main, high, x, moves, 0)
        start_all(rows_in)
        start, arrived = weight_copies(flags, at, own, other, held, sems)
        start((0, 1))
        wait_all(rows_in)
        for flag, first in ((2, 0), (3, 4)):

            @pl.when(flags[at, flag] == 1)
            def _():
                x[:, first : first + 2] = jnp.zeros_like(x[:, first : first + 2])

        def finish(rows, centre, keep_h, keep_d, mask):
            def one(frame, pre):
                gate = 1.0 / (1.0 + jnp.exp(-pre))
                slope = gate * (1.0 + pre * (1.0 - gate))
                value = centre[frame, 1 : 1 + rows].astype(jnp.float32) + pre * gate
                value = value.astype(jnp.bfloat16)
                if mask:
                    for row, flag in ((0, 2), (rows - 1, 3)):
                        keep_h[frame, row] = jnp.where(
                            flags[at, flag] == 1, jnp.zeros_like(value[row]), value[row]
                        )
                    keep_h[frame, 1 : rows - 1] = value[1 : rows - 1]
                else:
                    keep_h[frame] = value
                keep_d[frame] = slope.astype(jnp.bfloat16)

            return one

        spread(x, wide, (-1, 0, 1))
        convolve(wide, held, 0, 4, False, arrived, finish(4, x, ha, da, True))
        fields = sorted_copies(x.at[:, 1:5], ha, x_keep, x_send, moves, 3)
        start_sorted(fields, flags[at, 1])
        slope_a = pltpu.make_async_copy(da, da_out, moves.at[5])
        slope_a.start()
        spread(ha, wide_b, (-1, 0, 1))
        convolve(wide_b, held, 1, 2, False, arrived, finish(2, ha, hb, db, False))
        last = [
            pltpu.make_async_copy(hb, hb_out, moves.at[6]),
            pltpu.make_async_copy(db, db_out, moves.at[7]),
        ]
        start_all(last)
        results = sorted_copies(ha.at[:, 1:3], hb, out_keep, out_send, moves, 8)
        start_sorted(results, flags[at, 1])
        wait_all(last + [slope_a] + fields[0] + results[0])


def backward_kernel(
    at, flags, g_low, g_main, g_high, d_low, d_main, d_high, da_in, own, other, post_t, commit,
    quant_t,
    *refs,
):
    outs, scratch = refs[-17:-12], refs[-12:]
    pg_keep, pg_send, ig_keep, ig_send, iga_out = outs
    held, g, db, da, grad, small, plain, iga, wide, wide_b, sems, moves = scratch
    frames, rows6, cols, channels = g.shape

    @pl.when(flags[at, 0] == 1)
    def _():
        rows_in = place_rows(g_low, g_main, g_high, g, moves, 0)
        rows_in += place_rows(d_low, d_main, d_high, db, moves, 3)
        slope_in = pltpu.make_async_copy(da_in, da, moves.at[6])
        start_all(rows_in)
        start, arrived = weight_copies(flags, at, own, other, held, sems)
        start((1, 0))
        slope_in.start()
        wait_all(rows_in)

        def gate_in(source, slope, target, margin):
            rows = source.shape[1]

            def one(frame):
                for row in range(rows):
                    value = source[frame, row].astype(jnp.float32) * slope[frame, row].astype(
                        jnp.float32
                    )
                    value = value.astype(jnp.bfloat16)
                    if row < margin:
                        value = jnp.where(flags[at, 2] == 1, jnp.zeros_like(value), value)
                    if row >= rows - margin:
                        value = jnp.where(flags[at, 3] == 1, jnp.zeros_like(value), value)
                    target[frame, row] = value

            each(frames, one)

        gate_in(g, db, grad, 2)
        spread(grad, wide, (1, 0, -1))

        def plain_b(frame, sums):
            plain[frame] = (g[frame, 1:5].astype(jnp.float32) + sums).astype(jnp.bfloat16)

        convolve(wide, held, 1, 4, True, arrived, plain_b)
        slope_in.wait()
        gate_in(plain, da, small, 1)
        early = sorted_copies(small.at[:, 1:3], grad.at[:, 2:4], pg_keep, pg_send, moves, 7)
        start_sorted(early, flags[at, 1])
        spread(small, wide_b, (1, 0, -1))

        def plain_a(frame, sums):
            iga[frame] = (plain[frame, 1:3].astype(jnp.float32) + sums).astype(jnp.bfloat16)

        convolve(wide_b, held, 0, 2, True, arrived, plain_a)

        @pl.when(flags[at, 4] == 1)
        def _():
            whole = iga[...].reshape(frames * 2 * cols, channels)
            latent_grad = (
                jnp.dot(whole, post_t[...], preferred_element_type=jnp.float32) + commit[...]
            )
            back = jnp.dot(
                latent_grad.astype(jnp.bfloat16), quant_t[...], preferred_element_type=jnp.float32
            )
            iga[...] = back.astype(jnp.bfloat16).reshape(iga.shape)

        last = pltpu.make_async_copy(iga, iga_out, moves.at[11])
        last.start()
        results = sorted_copies(iga, plain.at[:, 1:3], ig_keep, ig_send, moves, 9)
        start_sorted(results, flags[at, 1])
        wait_all(early[0] + results[0] + [last])


def weight_grad_kernel(place, x_gathered, *refs):
    x_all, beside, total, moves = refs[-4:]
    out = refs[-5]
    count = len(refs) - 5
    pg_parts = refs[:count]
    clips, frames, rows, cols, channels = beside.shape[1:]
    micros = x_gathered.shape[1]
    pg_in, x_in, firsts = [], [], []
    first = 0
    for index, part in enumerate(pg_parts):
        length = part.shape[0]
        clip = slice(first, first + length)
        own_clip = slice(first % micros, first % micros + length)
        pg_in.append(pltpu.make_async_copy(part, beside.at[1, clip], moves.at[index]))
        x_in.append(
            pltpu.make_async_copy(
                x_gathered.at[place[2 + index], own_clip],
                x_all.at[clip, 2 : 2 + frames],
                moves.at[count + index],
            )
        )
        firsts.append(first)
        first += length
    start_all(pg_in + x_in)
    x_all[:, 0:2] = jnp.zeros_like(x_all[:, 0:2])
    for index, part in enumerate(pg_parts):
        pg_in[index].wait()

        def one(at):
            clip, frame = firsts[index] + at // frames, at % frames
            value = beside[1, clip, frame]
            beside[0, clip, frame] = shifted(value, 1)
            beside[2, clip, frame] = shifted(value, -1)

        each(part.shape[0] * frames, one)
    wait_all(x_in)

    def one_tap(number):
        tap = jnp.minimum(place[0] + number, 26)
        offset_t, offset_r, offset_c = tap // 9, (tap // 3) % 3, tap % 3
        depth = clips * frames * rows * cols
        lhs = x_all[:, pl.ds(offset_t, frames), pl.ds(offset_r, rows)].reshape(depth, channels)
        rhs = beside[offset_c].reshape(depth, channels)
        total[pl.ds(pl.multiple_of(number * channels, channels), channels), :] = lax.dot_general(
            lhs, rhs, (((0,), (0,)), ((), ())), preferred_element_type=jnp.float32
        )

    each(8, one_tap)
    begin = pl.multiple_of(place[1], 64)
    out[...] = total[pl.ds(begin, out.shape[0]), :].astype(jnp.bfloat16)


VMEM = pl.BlockSpec(memory_space=pltpu.VMEM)
SMEM = pl.BlockSpec(memory_space=pltpu.SMEM)
HBM = pl.BlockSpec(memory_space=pltpu.HBM)


def bf16(*shape):
    return jax.ShapeDtypeStruct(shape, jnp.bfloat16)


def cost(rows, cols, frames):
    flops = 2 * 27 * CH * CH * rows * cols * frames
    return pl.CostEstimate(flops=flops, bytes_accessed=4 * 27 * CH * CH, transcendentals=0)


def forward_pair(at, flags, rows, own, other, kept=()):
    frames, _, cols, channels = rows[1].shape
    depth = own.shape[0]
    four, two = (frames, 4, cols, channels), (frames, 2, cols, channels)
    return pl.pallas_call(
        functools.partial(forward_kernel, at),
        out_shape=tuple(bf16(*dims) for dims in (four, four, two, two, four, two, two)),
        in_specs=[SMEM] + [HBM] * (5 + len(kept)),
        out_specs=(HBM,) * 7,
        input_output_aliases={6 + index: index for index in range(len(kept))},
        scratch_shapes=[
            pltpu.VMEM((2, depth, channels), jnp.bfloat16),
            pltpu.VMEM((frames, 6, cols, channels), jnp.bfloat16),
            pltpu.VMEM(four, jnp.bfloat16),
            pltpu.VMEM(four, jnp.bfloat16),
            pltpu.VMEM(two, jnp.bfloat16),
            pltpu.VMEM(two, jnp.bfloat16),
            pltpu.VMEM((frames, 6, cols, WIDE), jnp.bfloat16),
            pltpu.VMEM((frames, 4, cols, WIDE), jnp.bfloat16),
            pltpu.SemaphoreType.DMA((2, 3)),
            pltpu.SemaphoreType.DMA((10,)),
        ],
        compiler_params=pltpu.CompilerParams(vmem_limit_bytes=56 * MIB),
        cost_estimate=cost(6, cols, frames),
    )(flags, *rows, own, other, *kept)


def backward_pair(at, flags, g_rows, d_rows, da, own, other, post_t, commit, quant_t, kept=()):
    frames, _, cols, channels = g_rows[1].shape
    depth = own.shape[0]
    six, four, two = ((frames, count, cols, channels) for count in (6, 4, 2))
    return pl.pallas_call(
        functools.partial(backward_kernel, at),
        out_shape=(bf16(*two),) * 5,
        in_specs=[SMEM] + [HBM] * 9 + [VMEM] * 3 + [HBM] * len(kept),
        out_specs=(HBM,) * 5,
        input_output_aliases={13 + index: index for index in range(len(kept))},
        scratch_shapes=[
            pltpu.VMEM((2, depth, channels), jnp.bfloat16),
            pltpu.VMEM(six, jnp.bfloat16),
            pltpu.VMEM(six, jnp.bfloat16),
            pltpu.VMEM(four, jnp.bfloat16),
            pltpu.VMEM(six, jnp.bfloat16),
            pltpu.VMEM(four, jnp.bfloat16),
            pltpu.VMEM(four, jnp.bfloat16),
            pltpu.VMEM(two, jnp.bfloat16),
            pltpu.VMEM((frames, 6, cols, WIDE), jnp.bfloat16),
            pltpu.VMEM((frames, 4, cols, WIDE), jnp.bfloat16),
            pltpu.SemaphoreType.DMA((2, 3)),
            pltpu.SemaphoreType.DMA((12,)),
        ],
        compiler_params=pltpu.CompilerParams(vmem_limit_bytes=56 * MIB),
        cost_estimate=cost(6, cols, frames),
    )(flags, *g_rows, *d_rows, da, own, other, post_t, commit, quant_t, *kept)


def weight_grad_part(place, x_gathered, pg_parts, depth):
    frames, rows, cols, channels = pg_parts[0].shape[1:]
    clips = sum(part.shape[0] for part in pg_parts)
    return pl.pallas_call(
        weight_grad_kernel,
        out_shape=bf16(depth, channels),
        in_specs=[SMEM] + [HBM] * (1 + len(pg_parts)),
        out_specs=VMEM,
        scratch_shapes=[
            pltpu.VMEM((clips, frames + 2, rows + 2, cols, channels), jnp.bfloat16),
            pltpu.VMEM((3, clips, frames, rows, cols, channels), jnp.bfloat16),
            pltpu.VMEM((8 * channels, channels), jnp.float32),
            pltpu.SemaphoreType.DMA((2 * len(pg_parts),)),
        ],
        compiler_params=pltpu.CompilerParams(vmem_limit_bytes=56 * MIB),
        cost_estimate=cost(2, cols, 2 * frames),
    )(place, x_gathered, *pg_parts)


def body(video_features, conv_weight, quant_weight, post_weight, latent_codes, cotangent):
    sections = lax.axis_size("section")
    slabs = lax.axis_size("slab")
    position = lax.axis_index("section")
    slab = lax.axis_index("slab")
    plane = position // 2
    core = position % 2
    planes = sections // 2
    middle = planes // 2
    micro_count, frames, row_count, cols, channels = video_features.shape
    bit_count = quant_weight.shape[1]

    def to_slab(value, step):
        return lax.ppermute(value, "slab", [(i, (i + step) % slabs) for i in range(slabs)])

    def to_core(value):
        return lax.ppermute(value, "section", [(i, i ^ 1) for i in range(sections)])

    def across(value, from_planes, plane_step, slab_step):
        pairs = []
        for at in from_planes:
            for half in range(2):
                for i in range(slabs):
                    target = i + slab_step
                    if 0 <= target < slabs:
                        source_section = 2 * at + half
                        target_section = 2 * (at + plane_step) + half
                        pairs.append(
                            (source_section * slabs + i, target_section * slabs + target)
                        )
        return lax.ppermute(value, BOTH, pairs)

    def beside(value):
        return to_slab(value, 1), value, to_slab(value, -1)

    def crossed(value, from_planes, plane_step, beside_it=()):
        main = across(value, from_planes, plane_step, 0)
        main, *rest = lax.optimization_barrier((main, *beside_it))
        return beside(main), rest

    own = conv_weight[0]
    other = to_core(own)

    codes = lax.dynamic_index_in_dim(latent_codes, core, 0, keepdims=False)
    bits = jnp.arange(32, dtype=jnp.int32)[:, None]
    flat_codes = codes.reshape(1, -1)
    sign_t = ((flat_codes >> bits) & 1).astype(jnp.float32) * 2.0 - 1.0
    sign_t = jnp.where(bits < bit_count, sign_t, 0.0)
    post_rows = jnp.pad(post_weight, ((0, 32 - bit_count), (0, 0)))
    dequant = (
        lax.dot_general(
            sign_t.astype(jnp.bfloat16),
            post_rows,
            (((0,), (0,)), ((), ())),
            preferred_element_type=jnp.float32,
        )
        .astype(jnp.bfloat16)
        .reshape(frames, row_count, cols, channels)
    )
    features = lax.dynamic_index_in_dim(video_features, core, 0, keepdims=False)
    upstream = lax.dynamic_index_in_dim(cotangent, core, 0, keepdims=False)
    entry = jnp.where(
        plane == middle, dequant, jnp.where(plane == planes - 1, upstream, features)
    )
    entry_rows = beside(entry)

    first_half = (plane % 2) == 0
    number = jnp.arange(planes + 2, dtype=jnp.int32)[:, None]
    active = jnp.where(
        number < planes, number == plane, (number == planes) == first_half
    )
    column = jnp.arange(5, dtype=jnp.int32)[None, :]
    flags = jnp.where(
        column == 0,
        active,
        jnp.where(
            column == 1,
            core == 1,
            jnp.where(
                column == 2,
                slab == 0,
                jnp.where(column == 3, slab == slabs - 1, plane == middle),
            ),
        ),
    ).astype(jnp.int32)
    flags, entry_rows = lax.optimization_barrier((flags, entry_rows))
    stage = forward_pair(planes, flags, entry_rows, own, other)
    own_late, other_late, post_late, quant_late, sign_late, _ = lax.optimization_barrier(
        (own, other, post_weight, quant_weight, sign_t, stage[5])
    )
    own_t, other_t = (
        value.reshape(27, channels, channels).swapaxes(1, 2).reshape(own.shape)
        for value in (own_late, other_late)
    )
    post_t = jnp.pad(post_late.T, ((0, 0), (0, LANES - bit_count)))
    quant_t = jnp.pad(quant_late.T, ((0, LANES - bit_count), (0, 0)))
    quant_wide = jnp.pad(quant_late, ((0, 0), (0, LANES - bit_count)))
    sign_rows = jnp.pad(sign_late.T, ((0, 0), (0, LANES - 32)))
    passed, late = crossed(
        stage[5], (0, 2), 1, (own_t, other_t, post_t, quant_t, quant_wide, sign_rows)
    )
    own_t, other_t, post_t, quant_t, quant_wide, sign_rows = late
    stage = forward_pair(planes + 1, flags, passed, own, other, stage)
    x_keep, x_send, out_keep, out_send, da, hb, db = stage
    d_rows = beside(db)
    hb_late, _ = lax.optimization_barrier((hb, d_rows))
    encoded = across(hb_late, (middle - 1,), 1, 0)

    along_x, along_z = 4, slabs // 4

    def mine(keep, send):
        got = to_core(send)
        return jnp.stack([jnp.where(core == 0, keep, got), jnp.where(core == 0, got, keep)])

    def along_ring(value):
        def moved(part, step):
            route = [(i, (i + step * along_z) % slabs) for i in range(slabs)]
            return lax.ppermute(part, "slab", route)

        below, above = moved(value, 1), moved(value, along_x - 1)
        half = micro_count // 2
        return [value, below, above, moved(below[:half], 1), moved(above[half:], along_x - 1)]

    x_groups = [[x * along_z + z for x in range(along_x)] for z in range(along_z)]
    latent = jnp.dot(
        encoded.reshape(-1, channels), quant_wide, preferred_element_type=jnp.float32
    )
    commit = 2.0 * COMMIT * (latent - sign_rows)

    g_rows = entry_rows
    kept = ()
    for at in range(planes - 1, -1, -1):
        kept = backward_pair(
            at, flags, g_rows, d_rows, da, own_t, other_t, post_t, commit, quant_t, kept
        )
        if at > 0:
            g_rows, _ = crossed(kept[4], (at,), -1)
        if at == planes - 1:
            x_keep, x_send, _ = lax.optimization_barrier((x_keep, x_send, kept[4]))
            x_all = lax.all_gather(
                jnp.stack([x_keep, to_core(x_send)]), "slab", axis_index_groups=x_groups
            )
    pg_keep, pg_send, ig_keep, ig_send, _ = kept

    pg_parts = along_ring(jnp.stack([pg_keep, to_core(pg_send)]))
    section_output = mine(out_keep, out_send)
    input_grad = mine(ig_keep, ig_send)
    depth = own.shape[0] // along_x
    first_row = (slab // along_z) * depth
    sources = [(slab // along_z + along_x - step) % along_x for step in (0, 1, along_x - 1, 2, 2)]
    place = jnp.stack([first_row // channels, first_row % channels] + sources).astype(jnp.int32)
    share = weight_grad_part(place, x_all, pg_parts, depth)
    blocks = share.reshape(along_z, depth // along_z, channels)
    at_z = slab % along_z
    total = lax.dynamic_index_in_dim(blocks, at_z, 0, keepdims=False).astype(jnp.float32)
    for step in (4, 3, 5, 2, 6, 1, 7):
        block = lax.dynamic_index_in_dim(blocks, (at_z + step) % along_z, 0, keepdims=False)
        route = [
            (i, i - i % along_z + (i % along_z + step) % along_z) for i in range(slabs)
        ]
        total = total + lax.ppermute(block, "slab", route).astype(jnp.float32)
    share = total
    return (section_output[None], input_grad[None], share[None])


def solution(mesh):
    return jax.shard_map(
        body,
        mesh=mesh,
        in_specs=(
            P(None, None, "slab", None, None),
            P("section", None, None),
            P(),
            P(),
            P(None, None, "slab", None),
            P(None, None, "slab", None, None),
        ),
        out_specs=(
            P("section", None, None, "slab", None, None),
            P("section", None, None, "slab", None, None),
            P("section", "slab", None),
        ),
        check_vma=False,
    )
```

```python
import functools

import jax
import jax.numpy as jnp
from jax import lax
from jax.experimental import pallas as pl
from jax.experimental.pallas import tpu as pltpu
from jax.sharding import PartitionSpec as P

COMMIT = 0.25
BOTH = ("section", "slab")
CH = 256
WIDE = 3 * CH
LANES = 128
MIB = 1024 * 1024


def shifted(value, step):
    count, cols, channels = value.shape
    flat = value.astype(jnp.float32).reshape(count * cols, channels)
    rolled = pltpu.roll(flat, (-step) % (count * cols), 0)
    column = lax.broadcasted_iota(jnp.int32, (count * cols, 1), 0) % cols
    inside = column != (cols - 1 if step == 1 else 0)
    return jnp.where(inside, rolled, 0.0).astype(jnp.bfloat16).reshape(value.shape)


def each(count, function):
    def step(index, carry):
        function(index)
        return carry

    lax.fori_loop(0, count, step, 0)


def spread(source, target, steps):
    def one(frame):
        value = source[frame]
        for third, step in enumerate(steps):
            target[frame, :, :, third * CH : (third + 1) * CH] = (
                value if step == 0 else shifted(value, step)
            )

    each(source.shape[0], one)


def convolve(wide, weights, layer, rows, flipped, arrived, consume):
    frames, _, cols, _ = wide.shape
    order = range(frames - 1, -1, -1) if flipped else range(frames)
    for step, frame in enumerate(order):
        if step < 3:
            arrived(layer, 2 - step)
        first_t = max(0, 2 - step)
        pieces = []
        for offset_t in range(first_t, 3):
            source = frame - offset_t + 2 if flipped else frame + offset_t - 2
            for offset_r in range(3):
                begin = 2 - offset_r if flipped else offset_r
                pieces.append(wide[source, begin : begin + rows].reshape(rows * cols, WIDE))
        sums = jnp.dot(
            jnp.concatenate(pieces, axis=-1),
            weights[layer, first_t * 3 * WIDE : 9 * WIDE, :],
            preferred_element_type=jnp.float32,
        )
        consume(frame, sums.reshape(rows, cols, CH))


def weight_copies(flags, at, own, other, held, sems, order):
    queue = [(layer, offset_t) for layer in order for offset_t in (2, 1, 0)]

    def copy(source, layer, offset_t):
        part = pl.ds(offset_t * 3 * WIDE, 3 * WIDE)
        return pltpu.make_async_copy(
            source.at[part], held.at[layer, part], sems.at[layer, offset_t]
        )

    def start(index):
        if index < len(queue):
            for source, wanted in ((own, True), (other, False)):

                @pl.when((flags[at, 1] == queue[index][0]) == wanted)
                def _():
                    copy(source, *queue[index]).start()

    def arrived(layer, offset_t):
        copy(own, layer, offset_t).wait()
        start(queue.index((layer, offset_t)) + 2)

    return start, arrived


def place_rows(low, main, high, target, sems, first):
    return [
        pltpu.make_async_copy(source, target.at[:, 2 * index : 2 * index + 2], sems.at[first + index])
        for index, source in enumerate((low, main, high))
    ]


def sorted_copies(first, second, keep, send, sems, at):
    return [
        [
            pltpu.make_async_copy(first, target, sems.at[at]),
            pltpu.make_async_copy(second, partner, sems.at[at + 1]),
        ]
        for target, partner in ((keep, send), (send, keep))
    ]


def start_sorted(choices, core):
    for index, copies in enumerate(choices):

        @pl.when(core == index)
        def _():
            start_all(copies)


def start_all(copies):
    for copy in copies:
        copy.start()


def wait_all(copies):
    for copy in copies:
        copy.wait()


def forward_kernel(at, flags, low, main, high, own, other, *refs):
    outs, scratch = refs[-17:-10], refs[-10:]
    x_keep, x_send, out_keep, out_send, da_out, hb_out, db_out = outs
    held, x, ha, da, hb, db, wide, wide_b, sems, moves = scratch

    @pl.when(flags[at, 0] == 1)
    def _():
        rows_in = place_rows(low, main, high, x, moves, 0)
        start_all(rows_in)
        start, arrived = weight_copies(flags, at, own, other, held, sems, (0, 1))
        start(0)
        wait_all(rows_in)
        start(1)
        for flag, first in ((2, 0), (3, 4)):

            @pl.when(flags[at, flag] == 1)
            def _():
                x[:, first : first + 2] = jnp.zeros_like(x[:, first : first + 2])

        def finish(rows, centre, keep_h, keep_d, mask):
            def one(frame, pre):
                gate = 1.0 / (1.0 + jnp.exp(-pre))
                slope = gate * (1.0 + pre * (1.0 - gate))
                value = centre[frame, 1 : 1 + rows].astype(jnp.float32) + pre * gate
                value = value.astype(jnp.bfloat16)
                if mask:
                    for row, flag in ((0, 2), (rows - 1, 3)):
                        keep_h[frame, row] = jnp.where(
                            flags[at, flag] == 1, jnp.zeros_like(value[row]), value[row]
                        )
                    keep_h[frame, 1 : rows - 1] = value[1 : rows - 1]
                else:
                    keep_h[frame] = value
                keep_d[frame] = slope.astype(jnp.bfloat16)

            return one

        spread(x, wide, (-1, 0, 1))
        convolve(wide, held, 0, 4, False, arrived, finish(4, x, ha, da, True))
        fields = sorted_copies(x.at[:, 1:5], ha, x_keep, x_send, moves, 3)
        start_sorted(fields, flags[at, 1])
        slope_a = pltpu.make_async_copy(da, da_out, moves.at[5])
        slope_a.start()
        spread(ha, wide_b, (-1, 0, 1))
        convolve(wide_b, held, 1, 2, False, arrived, finish(2, ha, hb, db, False))
        last = [
            pltpu.make_async_copy(hb, hb_out, moves.at[6]),
            pltpu.make_async_copy(db, db_out, moves.at[7]),
        ]
        start_all(last)
        results = sorted_copies(ha.at[:, 1:3], hb, out_keep, out_send, moves, 8)
        start_sorted(results, flags[at, 1])
        wait_all(last + [slope_a] + fields[0] + results[0])


def backward_kernel(
    at, flags, g_low, g_main, g_high, d_low, d_main, d_high, da_in, own, other, post_t, commit,
    quant_t,
    *refs,
):
    outs, scratch = refs[-17:-12], refs[-12:]
    pg_keep, pg_send, ig_keep, ig_send, iga_out = outs
    held, g, db, da, grad, small, plain, iga, wide, wide_b, sems, moves = scratch
    frames, rows6, cols, channels = g.shape

    @pl.when(flags[at, 0] == 1)
    def _():
        rows_in = place_rows(g_low, g_main, g_high, g, moves, 0)
        rows_in += place_rows(d_low, d_main, d_high, db, moves, 3)
        slope_in = pltpu.make_async_copy(da_in, da, moves.at[6])
        start_all(rows_in)
        start, arrived = weight_copies(flags, at, own, other, held, sems, (1, 0))
        start(0)
        wait_all(rows_in)
        start(1)
        slope_in.start()

        def gate_in(source, slope, target, margin):
            rows = source.shape[1]

            def one(frame):
                for row in range(rows):
                    value = source[frame, row].astype(jnp.float32) * slope[frame, row].astype(
                        jnp.float32
                    )
                    value = value.astype(jnp.bfloat16)
                    if row < margin:
                        value = jnp.where(flags[at, 2] == 1, jnp.zeros_like(value), value)
                    if row >= rows - margin:
                        value = jnp.where(flags[at, 3] == 1, jnp.zeros_like(value), value)
                    target[frame, row] = value

            each(frames, one)

        gate_in(g, db, grad, 2)
        spread(grad, wide, (1, 0, -1))

        def plain_b(frame, sums):
            plain[frame] = (g[frame, 1:5].astype(jnp.float32) + sums).astype(jnp.bfloat16)

        convolve(wide, held, 1, 4, True, arrived, plain_b)
        slope_in.wait()
        gate_in(plain, da, small, 1)
        early = sorted_copies(small.at[:, 1:3], grad.at[:, 2:4], pg_keep, pg_send, moves, 7)
        start_sorted(early, flags[at, 1])
        spread(small, wide_b, (1, 0, -1))

        def plain_a(frame, sums):
            iga[frame] = (plain[frame, 1:3].astype(jnp.float32) + sums).astype(jnp.bfloat16)

        convolve(wide_b, held, 0, 2, True, arrived, plain_a)

        @pl.when(flags[at, 4] == 1)
        def _():
            whole = iga[...].reshape(frames * 2 * cols, channels)
            latent_grad = (
                jnp.dot(whole, post_t[...], preferred_element_type=jnp.float32) + commit[...]
            )
            back = jnp.dot(
                latent_grad.astype(jnp.bfloat16), quant_t[...], preferred_element_type=jnp.float32
            )
            iga[...] = back.astype(jnp.bfloat16).reshape(iga.shape)

        last = pltpu.make_async_copy(iga, iga_out, moves.at[11])
        last.start()
        results = sorted_copies(iga, plain.at[:, 1:3], ig_keep, ig_send, moves, 9)
        start_sorted(results, flags[at, 1])
        wait_all(early[0] + results[0] + [last])


def weight_grad_kernel(place, x_first, x_second, *refs):
    x_all, beside, total, moves = refs[-4:]
    out = refs[-5]
    count = len(refs) - 5
    pg_parts = refs[:count]
    clips, frames, rows, cols, channels = beside.shape[1:]
    pg_in, x_in, firsts = [], [], []
    first = 0
    for index, part in enumerate(pg_parts):
        length = part.shape[0]
        clip = slice(first, first + length)
        pg_in.append(pltpu.make_async_copy(part, beside.at[1, clip], moves.at[index]))
        for number in range(first, first + length):
            source = (x_first, x_second)[number % 2]
            x_in.append(
                pltpu.make_async_copy(
                    source.at[place[2 + index]],
                    x_all.at[number, 2 : 2 + frames],
                    moves.at[count + number],
                )
            )
        firsts.append(first)
        first += length
    start_all(pg_in + x_in)
    x_all[:, 0:2] = jnp.zeros_like(x_all[:, 0:2])
    for index, part in enumerate(pg_parts):
        pg_in[index].wait()

        def one(at):
            clip, frame = firsts[index] + at // frames, at % frames
            value = beside[1, clip, frame]
            beside[0, clip, frame] = shifted(value, 1)
            beside[2, clip, frame] = shifted(value, -1)

        each(part.shape[0] * frames, one)
    wait_all(x_in)

    def one_tap(number):
        tap = jnp.minimum(place[0] + number, 26)
        offset_t, offset_r, offset_c = tap // 9, (tap // 3) % 3, tap % 3
        depth = clips * frames * rows * cols
        lhs = x_all[:, pl.ds(offset_t, frames), pl.ds(offset_r, rows)].reshape(depth, channels)
        rhs = beside[offset_c].reshape(depth, channels)
        total[pl.ds(pl.multiple_of(number * channels, channels), channels), :] = lax.dot_general(
            lhs, rhs, (((0,), (0,)), ((), ())), preferred_element_type=jnp.float32
        )

    each(8, one_tap)
    begin = pl.multiple_of(place[1], 64)
    out[...] = total[pl.ds(begin, out.shape[0]), :].astype(jnp.bfloat16)


VMEM = pl.BlockSpec(memory_space=pltpu.VMEM)
SMEM = pl.BlockSpec(memory_space=pltpu.SMEM)
HBM = pl.BlockSpec(memory_space=pltpu.HBM)


def bf16(*shape):
    return jax.ShapeDtypeStruct(shape, jnp.bfloat16)


def cost(rows, cols, frames):
    flops = 2 * 27 * CH * CH * rows * cols * frames
    return pl.CostEstimate(flops=flops, bytes_accessed=4 * 27 * CH * CH, transcendentals=0)


def forward_pair(at, flags, rows, own, other, kept=()):
    frames, _, cols, channels = rows[1].shape
    depth = own.shape[0]
    four, two = (frames, 4, cols, channels), (frames, 2, cols, channels)
    return pl.pallas_call(
        functools.partial(forward_kernel, at),
        out_shape=tuple(bf16(*dims) for dims in (four, four, two, two, four, two, two)),
        in_specs=[SMEM] + [HBM] * (5 + len(kept)),
        out_specs=(HBM,) * 7,
        input_output_aliases={6 + index: index for index in range(len(kept))},
        scratch_shapes=[
            pltpu.VMEM((2, depth, channels), jnp.bfloat16),
            pltpu.VMEM((frames, 6, cols, channels), jnp.bfloat16),
            pltpu.VMEM(four, jnp.bfloat16),
            pltpu.VMEM(four, jnp.bfloat16),
            pltpu.VMEM(two, jnp.bfloat16),
            pltpu.VMEM(two, jnp.bfloat16),
            pltpu.VMEM((frames, 6, cols, WIDE), jnp.bfloat16),
            pltpu.VMEM((frames, 4, cols, WIDE), jnp.bfloat16),
            pltpu.SemaphoreType.DMA((2, 3)),
            pltpu.SemaphoreType.DMA((10,)),
        ],
        compiler_params=pltpu.CompilerParams(vmem_limit_bytes=56 * MIB),
        cost_estimate=cost(6, cols, frames),
    )(flags, *rows, own, other, *kept)


def backward_pair(at, flags, g_rows, d_rows, da, own, other, post_t, commit, quant_t, kept=()):
    frames, _, cols, channels = g_rows[1].shape
    depth = own.shape[0]
    six, four, two = ((frames, count, cols, channels) for count in (6, 4, 2))
    return pl.pallas_call(
        functools.partial(backward_kernel, at),
        out_shape=(bf16(*two),) * 5,
        in_specs=[SMEM] + [HBM] * 9 + [VMEM] * 3 + [HBM] * len(kept),
        out_specs=(HBM,) * 5,
        input_output_aliases={13 + index: index for index in range(len(kept))},
        scratch_shapes=[
            pltpu.VMEM((2, depth, channels), jnp.bfloat16),
            pltpu.VMEM(six, jnp.bfloat16),
            pltpu.VMEM(six, jnp.bfloat16),
            pltpu.VMEM(four, jnp.bfloat16),
            pltpu.VMEM(six, jnp.bfloat16),
            pltpu.VMEM(four, jnp.bfloat16),
            pltpu.VMEM(four, jnp.bfloat16),
            pltpu.VMEM(two, jnp.bfloat16),
            pltpu.VMEM((frames, 6, cols, WIDE), jnp.bfloat16),
            pltpu.VMEM((frames, 4, cols, WIDE), jnp.bfloat16),
            pltpu.SemaphoreType.DMA((2, 3)),
            pltpu.SemaphoreType.DMA((12,)),
        ],
        compiler_params=pltpu.CompilerParams(vmem_limit_bytes=56 * MIB),
        cost_estimate=cost(6, cols, frames),
    )(flags, *g_rows, *d_rows, da, own, other, post_t, commit, quant_t, *kept)


def weight_grad_part(place, x_gathered, pg_parts, depth):
    frames, rows, cols, channels = pg_parts[0].shape[1:]
    clips = sum(part.shape[0] for part in pg_parts)
    return pl.pallas_call(
        weight_grad_kernel,
        out_shape=bf16(depth, channels),
        in_specs=[SMEM] + [HBM] * (2 + len(pg_parts)),
        out_specs=VMEM,
        scratch_shapes=[
            pltpu.VMEM((clips, frames + 2, rows + 2, cols, channels), jnp.bfloat16),
            pltpu.VMEM((3, clips, frames, rows, cols, channels), jnp.bfloat16),
            pltpu.VMEM((8 * channels, channels), jnp.float32),
            pltpu.SemaphoreType.DMA((len(pg_parts) + clips,)),
        ],
        compiler_params=pltpu.CompilerParams(vmem_limit_bytes=56 * MIB),
        cost_estimate=cost(2, cols, 2 * frames),
    )(place, *x_gathered, *pg_parts)


def body(video_features, conv_weight, quant_weight, post_weight, latent_codes, cotangent):
    sections = lax.axis_size("section")
    slabs = lax.axis_size("slab")
    position = lax.axis_index("section")
    slab = lax.axis_index("slab")
    plane = position // 2
    core = position % 2
    planes = sections // 2
    middle = planes // 2
    micro_count, frames, row_count, cols, channels = video_features.shape
    bit_count = quant_weight.shape[1]

    def to_slab(value, step):
        return lax.ppermute(value, "slab", [(i, (i + step) % slabs) for i in range(slabs)])

    def to_core(value):
        return lax.ppermute(value, "section", [(i, i ^ 1) for i in range(sections)])

    def across(value, from_planes, plane_step, slab_step):
        pairs = []
        for at in from_planes:
            for half in range(2):
                for i in range(slabs):
                    target = i + slab_step
                    if 0 <= target < slabs:
                        source_section = 2 * at + half
                        target_section = 2 * (at + plane_step) + half
                        pairs.append(
                            (source_section * slabs + i, target_section * slabs + target)
                        )
        return lax.ppermute(value, BOTH, pairs)

    def beside(value):
        return to_slab(value, 1), value, to_slab(value, -1)

    def crossed(value, from_planes, plane_step, beside_it=()):
        main = across(value, from_planes, plane_step, 0)
        main, *rest = lax.optimization_barrier((main, *beside_it))
        return beside(main), rest

    own = conv_weight[0]
    other = to_core(own)

    codes = lax.dynamic_index_in_dim(latent_codes, core, 0, keepdims=False)
    bits = jnp.arange(32, dtype=jnp.int32)[:, None]
    flat_codes = codes.reshape(1, -1)
    sign_t = ((flat_codes >> bits) & 1).astype(jnp.float32) * 2.0 - 1.0
    sign_t = jnp.where(bits < bit_count, sign_t, 0.0)
    post_rows = jnp.pad(post_weight, ((0, 32 - bit_count), (0, 0)))
    dequant = (
        lax.dot_general(
            sign_t.astype(jnp.bfloat16),
            post_rows,
            (((0,), (0,)), ((), ())),
            preferred_element_type=jnp.float32,
        )
        .astype(jnp.bfloat16)
        .reshape(frames, row_count, cols, channels)
    )
    features = lax.dynamic_index_in_dim(video_features, core, 0, keepdims=False)
    upstream = lax.dynamic_index_in_dim(cotangent, core, 0, keepdims=False)
    entry = jnp.where(
        plane == middle, dequant, jnp.where(plane == planes - 1, upstream, features)
    )
    entry_rows = beside(entry)

    first_half = (plane % 2) == 0
    number = jnp.arange(planes + 2, dtype=jnp.int32)[:, None]
    active = jnp.where(
        number < planes, number == plane, (number == planes) == first_half
    )
    column = jnp.arange(5, dtype=jnp.int32)[None, :]
    flags = jnp.where(
        column == 0,
        active,
        jnp.where(
            column == 1,
            core == 1,
            jnp.where(
                column == 2,
                slab == 0,
                jnp.where(column == 3, slab == slabs - 1, plane == middle),
            ),
        ),
    ).astype(jnp.int32)
    flags, entry_rows = lax.optimization_barrier((flags, entry_rows))
    stage = forward_pair(planes, flags, entry_rows, own, other)
    own_late, other_late, post_late, quant_late, sign_late, _ = lax.optimization_barrier(
        (own, other, post_weight, quant_weight, sign_t, stage[5])
    )
    own_t, other_t = (
        value.reshape(27, channels, channels).swapaxes(1, 2).reshape(own.shape)
        for value in (own_late, other_late)
    )
    post_t = jnp.pad(post_late.T, ((0, 0), (0, LANES - bit_count)))
    quant_t = jnp.pad(quant_late.T, ((0, LANES - bit_count), (0, 0)))
    quant_wide = jnp.pad(quant_late, ((0, 0), (0, LANES - bit_count)))
    sign_rows = jnp.pad(sign_late.T, ((0, 0), (0, LANES - 32)))
    passed, late = crossed(
        stage[5], (0, 2), 1, (own_t, other_t, post_t, quant_t, quant_wide, sign_rows)
    )
    own_t, other_t, post_t, quant_t, quant_wide, sign_rows = late
    stage = forward_pair(planes + 1, flags, passed, own, other, stage)
    x_keep, x_send, out_keep, out_send, da, hb, db = stage
    d_rows = beside(db)
    d_rows, x_got = lax.optimization_barrier((d_rows, to_core(x_send)))
    hb_late, _ = lax.optimization_barrier((hb, d_rows))
    encoded = across(hb_late, (middle - 1,), 1, 0)

    along_x, along_z = 4, slabs // 4

    def mine(keep, send):
        got = to_core(send)
        return jnp.stack([jnp.where(core == 0, keep, got), jnp.where(core == 0, got, keep)])

    def along_ring(value):
        def moved(part, step):
            route = [(i, (i + step * along_z) % slabs) for i in range(slabs)]
            return lax.ppermute(part, "slab", route)

        below, above = moved(value, 1), moved(value, along_x - 1)
        half = micro_count // 2
        return [value, below, above, moved(below[:half], 1), moved(above[half:], along_x - 1)]

    x_groups = [[x * along_z + z for x in range(along_x)] for z in range(along_z)]
    latent = jnp.dot(
        encoded.reshape(-1, channels), quant_wide, preferred_element_type=jnp.float32
    )
    commit = 2.0 * COMMIT * (latent - sign_rows)

    g_rows = entry_rows
    kept = ()
    for at in range(planes - 1, -1, -1):
        kept = backward_pair(
            at, flags, g_rows, d_rows, da, own_t, other_t, post_t, commit, quant_t, kept
        )
        if at > 0:
            g_rows, _ = crossed(kept[4], (at,), -1)
        if at == planes - 1:
            x_keep, x_got, _ = lax.optimization_barrier((x_keep, x_got, kept[4]))
            x_all = [
                lax.all_gather(value, "slab", axis_index_groups=x_groups)
                for value in (x_keep, x_got)
            ]
    pg_keep, pg_send, ig_keep, ig_send, _ = kept

    pg_parts = along_ring(jnp.stack([pg_keep, to_core(pg_send)]))
    section_output = mine(out_keep, out_send)
    input_grad = mine(ig_keep, ig_send)
    depth = own.shape[0] // along_x
    first_row = (slab // along_z) * depth
    sources = [(slab // along_z + along_x - step) % along_x for step in (0, 1, along_x - 1, 2, 2)]
    place = jnp.stack([first_row // channels, first_row % channels] + sources).astype(jnp.int32)
    share = weight_grad_part(place, x_all, pg_parts, depth)
    blocks = share.reshape(along_z, depth // along_z, channels)
    at_z = slab % along_z
    total = lax.dynamic_index_in_dim(blocks, at_z, 0, keepdims=False).astype(jnp.float32)
    for step in (4, 3, 5, 2, 6, 1, 7):
        block = lax.dynamic_index_in_dim(blocks, (at_z + step) % along_z, 0, keepdims=False)
        route = [
            (i, i - i % along_z + (i % along_z + step) % along_z) for i in range(slabs)
        ]
        total = total + lax.ppermute(block, "slab", route).astype(jnp.float32)
    share = total
    return (section_output[None], input_grad[None], share[None])


def solution(mesh):
    return jax.shard_map(
        body,
        mesh=mesh,
        in_specs=(
            P(None, None, "slab", None, None),
            P("section", None, None),
            P(),
            P(),
            P(None, None, "slab", None),
            P(None, None, "slab", None, None),
        ),
        out_specs=(
            P("section", None, None, "slab", None, None),
            P("section", None, None, "slab", None, None),
            P("section", "slab", None),
        ),
        check_vma=False,
    )
```

```python
import functools

import jax
import jax.numpy as jnp
from jax import lax
from jax.experimental import pallas as pl
from jax.experimental.pallas import tpu as pltpu
from jax.sharding import PartitionSpec as P

COMMIT = 0.25
BOTH = ("section", "slab")
CH = 256
WIDE = 3 * CH
LANES = 128
MIB = 1024 * 1024


def shifted(value, step):
    count, cols, channels = value.shape
    flat = value.astype(jnp.float32).reshape(count * cols, channels)
    rolled = pltpu.roll(flat, (-step) % (count * cols), 0)
    column = lax.broadcasted_iota(jnp.int32, (count * cols, 1), 0) % cols
    inside = column != (cols - 1 if step == 1 else 0)
    return jnp.where(inside, rolled, 0.0).astype(jnp.bfloat16).reshape(value.shape)


def each(count, function):
    def step(index, carry):
        function(index)
        return carry

    lax.fori_loop(0, count, step, 0)


def spread(source, target, steps):
    def one(frame):
        value = source[frame]
        for third, step in enumerate(steps):
            target[frame, :, :, third * CH : (third + 1) * CH] = (
                value if step == 0 else shifted(value, step)
            )

    each(source.shape[0], one)


def convolve(wide, weights, layer, rows, flipped, arrived, consume):
    frames, _, cols, _ = wide.shape
    order = range(frames - 1, -1, -1) if flipped else range(frames)
    for step, frame in enumerate(order):
        if step < 3:
            arrived(layer, 2 - step)
        first_t = max(0, 2 - step)
        pieces = []
        for offset_t in range(first_t, 3):
            source = frame - offset_t + 2 if flipped else frame + offset_t - 2
            for offset_r in range(3):
                begin = 2 - offset_r if flipped else offset_r
                pieces.append(wide[source, begin : begin + rows].reshape(rows * cols, WIDE))
        sums = jnp.dot(
            jnp.concatenate(pieces, axis=-1),
            weights[layer, first_t * 3 * WIDE : 9 * WIDE, :],
            preferred_element_type=jnp.float32,
        )
        consume(frame, sums.reshape(rows, cols, CH))


def weight_copies(flags, at, own, other, held, sems, order):
    queue = [(layer, offset_t) for layer in order for offset_t in (2, 1, 0)]

    def copy(source, layer, offset_t):
        part = pl.ds(offset_t * 3 * WIDE, 3 * WIDE)
        return pltpu.make_async_copy(
            source.at[part], held.at[layer, part], sems.at[layer, offset_t]
        )

    def start(index):
        if index < len(queue):
            for source, wanted in ((own, True), (other, False)):

                @pl.when((flags[at, 1] == queue[index][0]) == wanted)
                def _():
                    copy(source, *queue[index]).start()

    def arrived(layer, offset_t):
        copy(own, layer, offset_t).wait()
        start(queue.index((layer, offset_t)) + 2)

    return start, arrived


def place_rows(low, main, high, target, sems, first):
    return [
        pltpu.make_async_copy(source, target.at[:, 2 * index : 2 * index + 2], sems.at[first + index])
        for index, source in enumerate((low, main, high))
    ]


def sorted_copies(first, second, keep, send, sems, at):
    return [
        [
            pltpu.make_async_copy(first, target, sems.at[at]),
            pltpu.make_async_copy(second, partner, sems.at[at + 1]),
        ]
        for target, partner in ((keep, send), (send, keep))
    ]


def start_sorted(choices, core):
    for index, copies in enumerate(choices):

        @pl.when(core == index)
        def _():
            start_all(copies)


def start_all(copies):
    for copy in copies:
        copy.start()


def wait_all(copies):
    for copy in copies:
        copy.wait()


def forward_kernel(at, flags, low, main, high, own, other, *refs):
    outs, scratch = refs[-17:-10], refs[-10:]
    x_keep, x_send, out_keep, out_send, da_out, hb_out, db_out = outs
    held, x, ha, da, hb, db, wide, wide_b, sems, moves = scratch

    @pl.when(flags[at, 0] == 1)
    def _():
        rows_in = place_rows(low, main, high, x, moves, 0)
        start_all(rows_in)
        start, arrived = weight_copies(flags, at, own, other, held, sems, (0, 1))
        start(0)
        wait_all(rows_in)
        start(1)
        for flag, first in ((2, 0), (3, 4)):

            @pl.when(flags[at, flag] == 1)
            def _():
                x[:, first : first + 2] = jnp.zeros_like(x[:, first : first + 2])

        def finish(rows, centre, keep_h, keep_d, mask):
            def one(frame, pre):
                gate = 1.0 / (1.0 + jnp.exp(-pre))
                slope = gate * (1.0 + pre * (1.0 - gate))
                value = centre[frame, 1 : 1 + rows].astype(jnp.float32) + pre * gate
                value = value.astype(jnp.bfloat16)
                if mask:
                    for row, flag in ((0, 2), (rows - 1, 3)):
                        keep_h[frame, row] = jnp.where(
                            flags[at, flag] == 1, jnp.zeros_like(value[row]), value[row]
                        )
                    keep_h[frame, 1 : rows - 1] = value[1 : rows - 1]
                else:
                    keep_h[frame] = value
                keep_d[frame] = slope.astype(jnp.bfloat16)

            return one

        spread(x, wide, (-1, 0, 1))
        convolve(wide, held, 0, 4, False, arrived, finish(4, x, ha, da, True))
        fields = sorted_copies(x.at[:, 1:5], ha, x_keep, x_send, moves, 3)
        start_sorted(fields, flags[at, 1])
        slope_a = pltpu.make_async_copy(da, da_out, moves.at[5])
        slope_a.start()
        spread(ha, wide_b, (-1, 0, 1))
        convolve(wide_b, held, 1, 2, False, arrived, finish(2, ha, hb, db, False))
        last = [
            pltpu.make_async_copy(hb, hb_out, moves.at[6]),
            pltpu.make_async_copy(db, db_out, moves.at[7]),
        ]
        start_all(last)
        results = sorted_copies(ha.at[:, 1:3], hb, out_keep, out_send, moves, 8)
        start_sorted(results, flags[at, 1])
        wait_all(last + [slope_a] + fields[0] + results[0])


def backward_kernel(
    at, flags, g_low, g_main, g_high, d_low, d_main, d_high, da_in, own, other, post_t, commit,
    quant_t,
    *refs,
):
    outs, scratch = refs[-17:-12], refs[-12:]
    pg_keep, pg_send, ig_keep, ig_send, iga_out = outs
    held, g, db, da, grad, small, plain, iga, wide, wide_b, sems, moves = scratch
    frames, rows6, cols, channels = g.shape

    @pl.when(flags[at, 0] == 1)
    def _():
        rows_in = place_rows(g_low, g_main, g_high, g, moves, 0)
        rows_in += place_rows(d_low, d_main, d_high, db, moves, 3)
        slope_in = pltpu.make_async_copy(da_in, da, moves.at[6])
        start_all(rows_in)
        start, arrived = weight_copies(flags, at, own, other, held, sems, (1, 0))
        start(0)
        wait_all(rows_in)
        start(1)
        slope_in.start()

        def gate_in(source, slope, target, margin):
            rows = source.shape[1]

            def one(frame):
                for row in range(rows):
                    value = source[frame, row].astype(jnp.float32) * slope[frame, row].astype(
                        jnp.float32
                    )
                    value = value.astype(jnp.bfloat16)
                    if row < margin:
                        value = jnp.where(flags[at, 2] == 1, jnp.zeros_like(value), value)
                    if row >= rows - margin:
                        value = jnp.where(flags[at, 3] == 1, jnp.zeros_like(value), value)
                    target[frame, row] = value

            each(frames, one)

        gate_in(g, db, grad, 2)
        spread(grad, wide, (1, 0, -1))

        def plain_b(frame, sums):
            plain[frame] = (g[frame, 1:5].astype(jnp.float32) + sums).astype(jnp.bfloat16)

        convolve(wide, held, 1, 4, True, arrived, plain_b)
        slope_in.wait()
        gate_in(plain, da, small, 1)
        early = sorted_copies(small.at[:, 1:3], grad.at[:, 2:4], pg_keep, pg_send, moves, 7)
        start_sorted(early, flags[at, 1])
        spread(small, wide_b, (1, 0, -1))

        def plain_a(frame, sums):
            iga[frame] = (plain[frame, 1:3].astype(jnp.float32) + sums).astype(jnp.bfloat16)

        convolve(wide_b, held, 0, 2, True, arrived, plain_a)

        @pl.when(flags[at, 4] == 1)
        def _():
            whole = iga[...].reshape(frames * 2 * cols, channels)
            latent_grad = (
                jnp.dot(whole, post_t[...], preferred_element_type=jnp.float32) + commit[...]
            )
            back = jnp.dot(
                latent_grad.astype(jnp.bfloat16), quant_t[...], preferred_element_type=jnp.float32
            )
            iga[...] = back.astype(jnp.bfloat16).reshape(iga.shape)

        last = pltpu.make_async_copy(iga, iga_out, moves.at[11])
        last.start()
        results = sorted_copies(iga, plain.at[:, 1:3], ig_keep, ig_send, moves, 9)
        start_sorted(results, flags[at, 1])
        wait_all(early[0] + results[0] + [last])


def weight_grad_kernel(place, x_first, x_second, *refs):
    x_all, beside, total, moves = refs[-4:]
    out = refs[-5]
    count = len(refs) - 5
    pg_parts = refs[:count]
    clips, frames, rows, cols, channels = beside.shape[1:]
    pg_in, x_in, firsts = [], [], []
    first = 0
    for index, part in enumerate(pg_parts):
        length = part.shape[0]
        clip = slice(first, first + length)
        pg_in.append(pltpu.make_async_copy(part, beside.at[1, clip], moves.at[index]))
        for number in range(first, first + length):
            source = (x_first, x_second)[number % 2]
            x_in.append(
                pltpu.make_async_copy(
                    source.at[place[2 + index]],
                    x_all.at[number, 2 : 2 + frames],
                    moves.at[count + number],
                )
            )
        firsts.append(first)
        first += length
    start_all(pg_in + x_in)
    x_all[:, 0:2] = jnp.zeros_like(x_all[:, 0:2])
    for index, part in enumerate(pg_parts):
        pg_in[index].wait()

        def one(at):
            clip, frame = firsts[index] + at // frames, at % frames
            value = beside[1, clip, frame]
            beside[0, clip, frame] = shifted(value, 1)
            beside[2, clip, frame] = shifted(value, -1)

        each(part.shape[0] * frames, one)
    wait_all(x_in)

    def one_tap(number):
        tap = jnp.minimum(place[0] + number, 26)
        offset_t, offset_r, offset_c = tap // 9, (tap // 3) % 3, tap % 3
        depth = clips * frames * rows * cols
        lhs = x_all[:, pl.ds(offset_t, frames), pl.ds(offset_r, rows)].reshape(depth, channels)
        rhs = beside[offset_c].reshape(depth, channels)
        total[pl.ds(pl.multiple_of(number * channels, channels), channels), :] = lax.dot_general(
            lhs, rhs, (((0,), (0,)), ((), ())), preferred_element_type=jnp.float32
        )

    each(8, one_tap)
    begin = pl.multiple_of(place[1], 64)
    out[...] = total[pl.ds(begin, out.shape[0]), :].astype(jnp.bfloat16)


VMEM = pl.BlockSpec(memory_space=pltpu.VMEM)
SMEM = pl.BlockSpec(memory_space=pltpu.SMEM)
HBM = pl.BlockSpec(memory_space=pltpu.HBM)
ANY = pl.BlockSpec(memory_space=pl.ANY)


def bf16(*shape):
    return jax.ShapeDtypeStruct(shape, jnp.bfloat16)


def cost(rows, cols, frames):
    flops = 2 * 27 * CH * CH * rows * cols * frames
    return pl.CostEstimate(flops=flops, bytes_accessed=4 * 27 * CH * CH, transcendentals=0)


def forward_pair(at, flags, rows, own, other, kept=()):
    frames, _, cols, channels = rows[1].shape
    depth = own.shape[0]
    four, two = (frames, 4, cols, channels), (frames, 2, cols, channels)
    return pl.pallas_call(
        functools.partial(forward_kernel, at),
        out_shape=tuple(bf16(*dims) for dims in (four, four, two, two, four, two, two)),
        in_specs=[SMEM] + [ANY] * 3 + [HBM] * (2 + len(kept)),
        out_specs=(HBM,) * 7,
        input_output_aliases={6 + index: index for index in range(len(kept))},
        scratch_shapes=[
            pltpu.VMEM((2, depth, channels), jnp.bfloat16),
            pltpu.VMEM((frames, 6, cols, channels), jnp.bfloat16),
            pltpu.VMEM(four, jnp.bfloat16),
            pltpu.VMEM(four, jnp.bfloat16),
            pltpu.VMEM(two, jnp.bfloat16),
            pltpu.VMEM(two, jnp.bfloat16),
            pltpu.VMEM((frames, 6, cols, WIDE), jnp.bfloat16),
            pltpu.VMEM((frames, 4, cols, WIDE), jnp.bfloat16),
            pltpu.SemaphoreType.DMA((2, 3)),
            pltpu.SemaphoreType.DMA((10,)),
        ],
        compiler_params=pltpu.CompilerParams(vmem_limit_bytes=48 * MIB),
        cost_estimate=cost(6, cols, frames),
    )(flags, *rows, own, other, *kept)


def backward_pair(at, flags, g_rows, d_rows, da, own, other, post_t, commit, quant_t, kept=()):
    frames, _, cols, channels = g_rows[1].shape
    depth = own.shape[0]
    six, four, two = ((frames, count, cols, channels) for count in (6, 4, 2))
    return pl.pallas_call(
        functools.partial(backward_kernel, at),
        out_shape=(bf16(*two),) * 5,
        in_specs=[SMEM] + [ANY] * 6 + [HBM] * 3 + [VMEM] * 3 + [HBM] * len(kept),
        out_specs=(HBM,) * 5,
        input_output_aliases={13 + index: index for index in range(len(kept))},
        scratch_shapes=[
            pltpu.VMEM((2, depth, channels), jnp.bfloat16),
            pltpu.VMEM(six, jnp.bfloat16),
            pltpu.VMEM(six, jnp.bfloat16),
            pltpu.VMEM(four, jnp.bfloat16),
            pltpu.VMEM(six, jnp.bfloat16),
            pltpu.VMEM(four, jnp.bfloat16),
            pltpu.VMEM(four, jnp.bfloat16),
            pltpu.VMEM(two, jnp.bfloat16),
            pltpu.VMEM((frames, 6, cols, WIDE), jnp.bfloat16),
            pltpu.VMEM((frames, 4, cols, WIDE), jnp.bfloat16),
            pltpu.SemaphoreType.DMA((2, 3)),
            pltpu.SemaphoreType.DMA((12,)),
        ],
        compiler_params=pltpu.CompilerParams(vmem_limit_bytes=48 * MIB),
        cost_estimate=cost(6, cols, frames),
    )(flags, *g_rows, *d_rows, da, own, other, post_t, commit, quant_t, *kept)


def weight_grad_part(place, x_gathered, pg_parts, depth):
    frames, rows, cols, channels = pg_parts[0].shape[1:]
    clips = sum(part.shape[0] for part in pg_parts)
    return pl.pallas_call(
        weight_grad_kernel,
        out_shape=bf16(depth, channels),
        in_specs=[SMEM] + [HBM] * (2 + len(pg_parts)),
        out_specs=VMEM,
        scratch_shapes=[
            pltpu.VMEM((clips, frames + 2, rows + 2, cols, channels), jnp.bfloat16),
            pltpu.VMEM((3, clips, frames, rows, cols, channels), jnp.bfloat16),
            pltpu.VMEM((8 * channels, channels), jnp.float32),
            pltpu.SemaphoreType.DMA((len(pg_parts) + clips,)),
        ],
        compiler_params=pltpu.CompilerParams(vmem_limit_bytes=48 * MIB),
        cost_estimate=cost(2, cols, 2 * frames),
    )(place, *x_gathered, *pg_parts)


def body(video_features, conv_weight, quant_weight, post_weight, latent_codes, cotangent):
    sections = lax.axis_size("section")
    slabs = lax.axis_size("slab")
    position = lax.axis_index("section")
    slab = lax.axis_index("slab")
    plane = position // 2
    core = position % 2
    planes = sections // 2
    middle = planes // 2
    micro_count, frames, row_count, cols, channels = video_features.shape
    bit_count = quant_weight.shape[1]

    def to_slab(value, step):
        return lax.ppermute(value, "slab", [(i, (i + step) % slabs) for i in range(slabs)])

    def to_core(value):
        return lax.ppermute(value, "section", [(i, i ^ 1) for i in range(sections)])

    def across(value, from_planes, plane_step, slab_step):
        pairs = []
        for at in from_planes:
            for half in range(2):
                for i in range(slabs):
                    target = i + slab_step
                    if 0 <= target < slabs:
                        source_section = 2 * at + half
                        target_section = 2 * (at + plane_step) + half
                        pairs.append(
                            (source_section * slabs + i, target_section * slabs + target)
                        )
        return lax.ppermute(value, BOTH, pairs)

    def beside(value):
        return to_slab(value, 1), value, to_slab(value, -1)

    def crossed(value, from_planes, plane_step, beside_it=()):
        main = across(value, from_planes, plane_step, 0)
        main, *rest = lax.optimization_barrier((main, *beside_it))
        return beside(main), rest

    own = conv_weight[0]
    other = to_core(own)

    codes = lax.dynamic_index_in_dim(latent_codes, core, 0, keepdims=False)
    bits = jnp.arange(32, dtype=jnp.int32)[:, None]
    flat_codes = codes.reshape(1, -1)
    sign_t = ((flat_codes >> bits) & 1).astype(jnp.float32) * 2.0 - 1.0
    sign_t = jnp.where(bits < bit_count, sign_t, 0.0)
    post_rows = jnp.pad(post_weight, ((0, 32 - bit_count), (0, 0)))
    dequant = (
        lax.dot_general(
            sign_t.astype(jnp.bfloat16),
            post_rows,
            (((0,), (0,)), ((), ())),
            preferred_element_type=jnp.float32,
        )
        .astype(jnp.bfloat16)
        .reshape(frames, row_count, cols, channels)
    )
    features = lax.dynamic_index_in_dim(video_features, core, 0, keepdims=False)
    upstream = lax.dynamic_index_in_dim(cotangent, core, 0, keepdims=False)
    entry = jnp.where(
        plane == middle, dequant, jnp.where(plane == planes - 1, upstream, features)
    )
    entry_rows = beside(entry)

    first_half = (plane % 2) == 0
    number = jnp.arange(planes + 2, dtype=jnp.int32)[:, None]
    active = jnp.where(
        number < planes, number == plane, (number == planes) == first_half
    )
    column = jnp.arange(5, dtype=jnp.int32)[None, :]
    flags = jnp.where(
        column == 0,
        active,
        jnp.where(
            column == 1,
            core == 1,
            jnp.where(
                column == 2,
                slab == 0,
                jnp.where(column == 3, slab == slabs - 1, plane == middle),
            ),
        ),
    ).astype(jnp.int32)
    flags, entry_rows = lax.optimization_barrier((flags, entry_rows))
    stage = forward_pair(planes, flags, entry_rows, own, other)
    own_late, other_late, post_late, quant_late, sign_late, _ = lax.optimization_barrier(
        (own, other, post_weight, quant_weight, sign_t, stage[5])
    )
    own_t, other_t = (
        value.reshape(27, channels, channels).swapaxes(1, 2).reshape(own.shape)
        for value in (own_late, other_late)
    )
    post_t = jnp.pad(post_late.T, ((0, 0), (0, LANES - bit_count)))
    quant_t = jnp.pad(quant_late.T, ((0, LANES - bit_count), (0, 0)))
    quant_wide = jnp.pad(quant_late, ((0, 0), (0, LANES - bit_count)))
    sign_rows = jnp.pad(sign_late.T, ((0, 0), (0, LANES - 32)))
    passed, late = crossed(
        stage[5], (0, 2), 1, (own_t, other_t, post_t, quant_t, quant_wide, sign_rows)
    )
    own_t, other_t, post_t, quant_t, quant_wide, sign_rows = late
    stage = forward_pair(planes + 1, flags, passed, own, other, stage)
    x_keep, x_send, out_keep, out_send, da, hb, db = stage
    d_rows = beside(db)
    d_rows, x_got = lax.optimization_barrier((d_rows, to_core(x_send)))
    hb_late, _ = lax.optimization_barrier((hb, d_rows))
    encoded = across(hb_late, (middle - 1,), 1, 0)

    along_x, along_z = 4, slabs // 4

    def mine(keep, send):
        got = to_core(send)
        return jnp.stack([jnp.where(core == 0, keep, got), jnp.where(core == 0, got, keep)])

    def along_ring(value):
        def moved(part, step):
            route = [(i, (i + step * along_z) % slabs) for i in range(slabs)]
            return lax.ppermute(part, "slab", route)

        below, above = moved(value, 1), moved(value, along_x - 1)
        half = micro_count // 2
        return [value, below, above, moved(below[:half], 1), moved(above[half:], along_x - 1)]

    x_groups = [[x * along_z + z for x in range(along_x)] for z in range(along_z)]
    latent = jnp.dot(
        encoded.reshape(-1, channels), quant_wide, preferred_element_type=jnp.float32
    )
    commit = 2.0 * COMMIT * (latent - sign_rows)

    g_rows = entry_rows
    kept = ()
    for at in range(planes - 1, -1, -1):
        kept = backward_pair(
            at,
            flags,
            g_rows,
            d_rows,
            da,
            own_t,
            other_t,
            post_t,
            commit if at <= middle else sign_rows,
            quant_t,
            kept,
        )
        if at > 0:
            g_rows, _ = crossed(kept[4], (at,), -1)
        if at == planes - 1:
            x_keep, x_got, _ = lax.optimization_barrier((x_keep, x_got, kept[4]))
            x_all = [
                lax.all_gather(value, "slab", axis_index_groups=x_groups)
                for value in (x_keep, x_got)
            ]
    pg_keep, pg_send, ig_keep, ig_send, _ = kept

    pg_parts = along_ring(jnp.stack([pg_keep, to_core(pg_send)]))
    section_output = mine(out_keep, out_send)
    input_grad = mine(ig_keep, ig_send)
    depth = own.shape[0] // along_x
    first_row = (slab // along_z) * depth
    sources = [(slab // along_z + along_x - step) % along_x for step in (0, 1, along_x - 1, 2, 2)]
    place = jnp.stack([first_row // channels, first_row % channels] + sources).astype(jnp.int32)
    share = weight_grad_part(place, x_all, pg_parts, depth)
    blocks = share.reshape(along_z, depth // along_z, channels)
    at_z = slab % along_z
    total = lax.dynamic_index_in_dim(blocks, at_z, 0, keepdims=False).astype(jnp.float32)
    for step in (4, 3, 5, 2, 6, 1, 7):
        block = lax.dynamic_index_in_dim(blocks, (at_z + step) % along_z, 0, keepdims=False)
        route = [
            (i, i - i % along_z + (i % along_z + step) % along_z) for i in range(slabs)
        ]
        total = total + lax.ppermute(block, "slab", route).astype(jnp.float32)
    share = total
    return (section_output[None], input_grad[None], share[None])


def solution(mesh):
    return jax.shard_map(
        body,
        mesh=mesh,
        in_specs=(
            P(None, None, "slab", None, None),
            P("section", None, None),
            P(),
            P(),
            P(None, None, "slab", None),
            P(None, None, "slab", None, None),
        ),
        out_specs=(
            P("section", None, None, "slab", None, None),
            P("section", None, None, "slab", None, None),
            P("section", "slab", None),
        ),
        check_vma=False,
    )
```
